128 devices in a mesh: side: 2 (over z_hi), batch: 32 (over y, z_lo, x), mp: 2 (over core).
Axes of the slice: x: 4, y: 4, z: 4 (z_hi: 2, z_lo: 2; z = z_hi * 2 + z_lo), core: 2. Of those that a mesh axis runs over, the one named last changes fastest.
Arguments:
- hidden_in: bfloat16 [2, 49152, 768], P('side', 'batch'), may hold values from -6 to 6
- w_qkv: bfloat16 [2, 768, 3, 768], P('side', None, None, 'mp'), may hold values from -0.21875 to 0.21875
- b_qv: float32 [2, 2, 768], P('side', None, 'mp'), may hold values from -4 to 4
- w_out: bfloat16 [2, 768, 768], P('side', 'mp'), may hold values from -0.625 to 0.625
- b_out: float32 [2, 768], P('side'), may hold values from -4 to 4
- ln1_gain: float32 [2, 768], P('side'), may hold values from 0.5 to 1.5
- ln1_bias: float32 [2, 768], P('side'), may hold values from -4 to 4
- w_up: bfloat16 [2, 768, 3072], P('side', None, 'mp'), may hold values from -0.21875 to 0.21875
- b_up: float32 [2, 3072], P('side', 'mp'), may hold values from -6 to 6
- w_down: bfloat16 [2, 3072, 768], P('side', 'mp'), may hold values from -0.109375 to 0.109375
- b_down: float32 [2, 768], P('side'), may hold values from -4 to 4
- ln2_gain: float32 [2, 768], P('side'), may hold values from 0.5 to 1.5
- ln2_bias: float32 [2, 768], P('side'), may hold values from -4 to 4
- lengths: int32 [2, 768], P('side', 'batch'), may hold values from 0 to 64, as said below
- positives: int32 [768, 192], P('batch'), may hold values from 0 to 1, as said below
- out_grad: bfloat16 [2, 49152, 768], P('side', 'batch'), may hold values from -6 to 6
Outputs:
- encoded: bfloat16 [2, 49152, 768], P('side', 'batch')
- input_grad: bfloat16 [2, 49152, 768], P('side', 'batch')
- question_loss: float32 [768], P('batch')
- g_w_qkv: float32 [2, 768, 3, 768], P('side', 'batch', None, 'mp')
- g_b_qv: float32 [2, 2, 768], P('side', None, ('mp', 'batch'))
- g_w_out: float32 [2, 768, 768], P('side', ('mp', 'batch'))
- g_b_out: float32 [2, 768], P('side', 'batch')
- g_ln1_gain: float32 [2, 768], P('side', 'batch')
- g_ln1_bias: float32 [2, 768], P('side', 'batch')
- g_w_up: float32 [2, 768, 3072], P('side', 'batch', 'mp')
- g_b_up: float32 [2, 3072], P('side', ('mp', 'batch'))
- g_w_down: float32 [2, 3072, 768], P('side', ('mp', 'batch'))
- g_b_down: float32 [2, 768], P('side', 'batch')
- g_ln2_gain: float32 [2, 768], P('side', 'batch')
- g_ln2_bias: float32 [2, 768], P('side', 'batch')
The draws below stay inside these ranges and needn't reach their ends.
Inputs may be any that keep to these rules, and one draw needn't show every extreme that they name: `lengths`: on encoder 0 each entry is one question's live tokens, a prefix of at least 8, and the first question is full; on encoder 1 each run of 4 entries is one passage whose live tokens are a prefix of 64 to 256, and the first passage is full. `positives`: each row has between 1 and 4 ones; the first row has 4.
All inputs are finite; a program needn't handle non-finite values.
Results may differ from the reference program's by a relative error of at most 0.012.
Values may be sent and summed in bfloat16 or wider, within the bound.
A program may use at most 192 MiB of HBM per device.

```python
import jax
import jax.numpy as jnp
from jax import lax

D = 768
HEADS = 12
HDIM = 64
FF = 3072
QLEN = 64
PLEN = 256
TOKENS = 49152
NQ = 768
NP = 192


def draw_lengths(key, part):
    key = jax.random.fold_in(key, 11)
    first_key, second_key = jax.random.split(key)
    question_len = jax.random.randint(first_key, (NQ,), QLEN // 8, QLEN + 1)
    question_len = question_len.at[0].set(QLEN)
    passage_len = jax.random.randint(second_key, (NP,), QLEN, PLEN + 1)
    passage_len = passage_len.at[0].set(PLEN)
    slot_index = jnp.arange(PLEN // QLEN)
    passage_slots = jnp.clip(passage_len[:, None] - QLEN * slot_index[None, :], 0, QLEN).reshape(NQ)
    return jnp.stack([question_len, passage_slots]).astype(jnp.int32)


def draw_positives(key, part):
    key = jax.random.fold_in(key, 23)
    first_key, second_key = jax.random.split(key)
    picks = jax.random.randint(first_key, (NQ, 4), 0, NP)
    picks = picks.at[0].set(jnp.arange(4))
    counts = jax.random.randint(second_key, (NQ,), 1, 5)
    counts = counts.at[0].set(4)
    columns = jnp.arange(NP)
    hits = (picks[:, :, None] == columns[None, None, :]) & (jnp.arange(4)[None, :, None] < counts[:, None, None])
    return jnp.any(hits, axis=1).astype(jnp.int32)


def levels(key, shape, shards, smallest, top_value):
    loudness = 1.0
    for position, shards_of in shards:
        steps = jax.random.uniform(jax.random.fold_in(jax.random.fold_in(key, 6), position), (shards_of,), jnp.float32, smallest / len(shards), top_value / len(shards))
        loudness = loudness * jnp.repeat(jnp.exp(steps), shape[position] // shards_of).reshape((-1,) + (1,) * (len(shape) - 1 - position))
    return loudness


def gaussian(own_key, dims, scale, limit, shards=(), dtype=jnp.bfloat16):
    level = levels(own_key, dims, shards, -0.22, 0.18) if shards else 1.0
    array = jax.random.normal(own_key, dims, jnp.float32) * scale * level
    return jnp.minimum(jnp.maximum(array, -limit), limit).astype(dtype)


def setup_inputs(seed: int = 0) -> dict:
    streams_of = jax.random.split(jax.random.key(seed), 17)
    return {
        "hidden_in": gaussian(streams_of[0], (2, TOKENS, D), 1.0, 6.0, ((0, 2), (1, 32))),
        "w_qkv": gaussian(streams_of[1], (2, D, 3, D), D ** -0.5, 0.21875, ((0, 2), (3, 2))),
        "b_qv": gaussian(streams_of[2], (2, 2, D), 0.3, 4.0, ((0, 2), (2, 2)), jnp.float32),
        "w_out": gaussian(streams_of[3], (2, D, D), (D // 8) ** -0.5, 0.625, ((0, 2), (1, 2))),
        "b_out": gaussian(streams_of[4], (2, D), 0.3, 4.0, ((0, 2),), jnp.float32),
        "ln1_gain": jnp.clip(1.0 + 0.1 * jax.random.normal(streams_of[5], (2, D), jnp.float32), 0.5, 1.5),
        "ln1_bias": gaussian(streams_of[6], (2, D), 0.3, 4.0, ((0, 2),), jnp.float32),
        "w_up": gaussian(streams_of[7], (2, D, FF), D ** -0.5, 0.21875, ((0, 2), (2, 2))),
        "b_up": gaussian(streams_of[8], (2, FF), 0.5, 6.0, ((0, 2), (1, 2)), jnp.float32),
        "w_down": gaussian(streams_of[9], (2, FF, D), FF ** -0.5, 0.109375, ((0, 2), (1, 2))),
        "b_down": gaussian(streams_of[10], (2, D), 0.3, 4.0, ((0, 2),), jnp.float32),
        "ln2_gain": jnp.clip(1.0 + 0.1 * jax.random.normal(streams_of[11], (2, D), jnp.float32), 0.5, 1.5),
        "ln2_bias": gaussian(streams_of[12], (2, D), 0.3, 4.0, ((0, 2),), jnp.float32),
        "lengths": draw_lengths(jax.random.fold_in(streams_of[16], 71), 0),
        "positives": draw_positives(jax.random.fold_in(streams_of[16], 71), 0),
        "out_grad": gaussian(streams_of[15], (2, TOKENS, D), 1.0, 6.0, ((0, 2), (1, 32))),
    }


epsilon = 1e-05
sim_scale = 0.1
score_scale = 0.125

@jax.custom_vjp
def low(v):
    return lax.optimization_barrier(v.astype(jnp.bfloat16)).astype(jnp.float32)

@jax.custom_vjp
def low_back(v):
    return v

def low_keep(v):
    return (low(v), None)

def low_pass(kept, grad):
    return (grad,)

def back_keep(v):
    return (v, None)

def back_low(kept, grad):
    return (low(grad),)
low.defvjp(low_keep, low_pass)
low_back.defvjp(back_keep, back_low)

def matmul(left, right):
    return jnp.dot(left, right, precision=lax.Precision.HIGHEST, preferred_element_type=jnp.float32)

def layer_norm(values, gain, shift):
    centered = values - lax.optimization_barrier(jnp.mean(values, axis=-1, keepdims=True))
    spread = lax.optimization_barrier(jnp.mean(centered * centered, axis=-1, keepdims=True))
    return centered * lax.rsqrt(spread + epsilon) * gain + shift

def tile_attention(block):
    queries, key_rows, value_rows, key_masks = block
    scores = jnp.einsum('ihd,jhd->hij', queries, key_rows, precision=lax.Precision.HIGHEST) * score_scale
    scores = low_back(scores)
    scores = jnp.where(key_masks[None], scores, -1000000000.0)
    weights = low(jax.nn.softmax(scores, axis=-1))
    return jnp.einsum('hij,jhd->ihd', weights, value_rows, precision=lax.Precision.HIGHEST)

def live_rows(counts):
    return (jnp.arange(QLEN)[None, :] < counts[:, None]).reshape(-1)

def encoder(hidden, w_qkv, b_qv, w_out, b_out, ln1_gain, ln1_bias, w_up, b_up, w_down, b_down, ln2_gain, ln2_bias, live, seg_len):
    projected = matmul(hidden, w_qkv.reshape(D, 3 * D)).reshape(TOKENS, 3, D)
    queries = low(low_back(projected[:, 0] + b_qv[0]))
    key_rows = low(low_back(projected[:, 1]))
    value_rows = low(low_back(projected[:, 2] + b_qv[1]))
    positions = jnp.arange(PLEN)
    same_part = positions[:, None] // seg_len == positions[None, :] // seg_len
    key_masks = same_part[None] & live.reshape(NP, PLEN)[:, None, :]
    tile_shape = (NP, PLEN, HEADS, HDIM)
    context = lax.map(jax.checkpoint(tile_attention), (queries.reshape(tile_shape), key_rows.reshape(tile_shape), value_rows.reshape(tile_shape), key_masks))
    context = low(low_back(context.reshape(TOKENS, D)))
    attended = low_back(matmul(context, w_out))
    first = layer_norm(hidden + attended + b_out, ln1_gain, ln1_bias)
    up_value = low_back(matmul(low(first), w_up) + b_up)
    activated = low(jax.nn.gelu(up_value, approximate=False))
    feed_out = low_back(matmul(activated, w_down))
    return layer_norm(first + feed_out + b_down, ln2_gain, ln2_bias)

def reference(hidden_in, w_qkv, b_qv, w_out, b_out, ln1_gain, ln1_bias, w_up, b_up, w_down, b_down, ln2_gain, ln2_bias, lengths, positives, out_grad):
    primal = tuple((item.astype(jnp.float32) for item in (hidden_in, w_qkv, b_qv, w_out, b_out, ln1_gain, ln1_bias, w_up, b_up, w_down, b_down, ln2_gain, ln2_bias)))
    lives = [live_rows(lengths[0]), live_rows(lengths[1])]
    seg_lens = [QLEN, PLEN]

    def forward(*params):
        outputs = [encoder(*[item[which] for item in params], lives[which], seg_lens[which]) for which in range(2)]
        question_cls = low(outputs[0].reshape(NQ, QLEN, D)[:, 0])
        passage_cls = low(outputs[1].reshape(NP, PLEN, D)[:, 0])
        sims = matmul(question_cls, passage_cls.T) * sim_scale
        chosen = jnp.where(positives > 0, sims, -1000000000.0)
        losses = jax.nn.logsumexp(sims, axis=1) - jax.nn.logsumexp(chosen, axis=1)
        return (jnp.stack(outputs), losses)
    (encoded, losses), pullback = jax.vjp(forward, *primal)
    positions = jnp.arange(TOKENS)
    keeps = jnp.stack([lives[which] & (positions % seg_lens[which] != 0) for which in range(2)])
    cotangent = out_grad.astype(jnp.float32) * keeps[:, :, None].astype(jnp.float32)
    grads = pullback((cotangent, jnp.ones_like(losses)))
    return (encoded.astype(jnp.bfloat16), grads[0].astype(jnp.bfloat16), losses, grads[1], grads[2], grads[3], grads[4], grads[5], grads[6], grads[7], grads[8], grads[9], grads[10], grads[11], grads[12])
```

```python
import functools
import types

import jax
import jax.numpy as jnp
from jax import lax
from jax.experimental import pallas as pl
from jax.experimental.pallas import tpu as pltpu
from jax.sharding import PartitionSpec as P

MESH = pl.DeviceIdType.MESH
bf16 = jnp.bfloat16
f32 = jnp.float32
WIDTH = 768
HALF = 384
ROWS = 768
SLOT = 64
SLOTS = 12
PAIRS = 6
EPS = 1e-05
SIM_SCALE = 0.1
HIGH = lax.Precision.HIGHEST


def nn(a, b, precision=None):
    return lax.dot_general(a, b, (((1,), (0,)), ((), ())), precision=precision, preferred_element_type=f32)


def nt(a, b, precision=None):
    return lax.dot_general(a, b, (((1,), (1,)), ((), ())), precision=precision, preferred_element_type=f32)


def tn(a, b, precision=None):
    return lax.dot_general(a, b, (((0,), (0,)), ((), ())), precision=precision, preferred_element_type=f32)


def iota(shape, axis):
    return lax.broadcasted_iota(jnp.int32, shape, axis)


def split_pair(block):
    first = iota(block.shape, 1) < 64
    zero = jnp.zeros_like(block)
    return jnp.concatenate([jnp.where(first, block, zero), jnp.where(first, zero, block)], axis=0)


def merge_pair(stacked):
    rows = stacked.shape[0] // 2
    first = iota((rows, 128), 1) < 64
    return jnp.where(first, stacked[:rows], stacked[rows:])


def mean_of(values):
    return jnp.sum(values, axis=1, keepdims=True) * (1.0 / WIDTH)


def norm_back(d, n, gain, root):
    u = d * gain
    return (u - mean_of(u) - n * mean_of(u * n)) * root


def partial_sum(values):
    return jnp.sum(values.reshape(values.shape[0] // 8, 8, values.shape[1]), axis=0)


def column_sum(values):
    return jnp.sum(values, axis=0, keepdims=True)


class Counter:
    def __init__(self):
        self.n = 0

    def take(self):
        self.n += 1
        return self.n - 1


class Bundle:
    def __init__(self, rc, where, first, grad, r1, r2, r3, finish):
        self.rc, self.first, self.grad, self.finish = rc, first, grad, finish
        self.r1, self.r2, self.r3 = r1, r2, r3
        self.x, self.y, self.z, self.device = where
        self.a = self.y if first == "y" else self.x
        self.b = self.x if first == "y" else self.y
        self.last = grad.shape[2] if first == "y" else grad.shape[0]
        self.step = 0
        self.sent = []

    def index(self, a, z, b):
        return (a, z, b) if self.first == "y" else (b, z, a)

    def piece(self, a, z):
        return self.grad.at[a, z] if self.first == "y" else self.grad.at[:, z, a]

    def to(self, da, dz, db):
        return self.device(da, dz, db) if self.first == "y" else self.device(db, dz, da)

    def owner_b(self, b):
        return b if self.last == 4 else b // 2

    def send(self, src, dst, to):
        copy = self.rc(src, dst, to)
        copy.start()
        self.sent.append(copy)
        return copy

    def add(self, where, others):
        def step(b, carry):
            for part in range(self.grad.shape[3] // 16):
                rows = pl.ds(part * 16, 16)
                total = self.grad[where(b) + (rows,)].astype(f32)
                for ref, index in others(b):
                    total = total + ref[index + (rows,)].astype(f32)
                self.grad[where(b) + (rows,)] = total.astype(bf16)
            return carry

        lax.fori_loop(0, self.last, step, 0)

    def advance(self):
        (self.step0, self.step1, self.step2, self.step3)[self.step]()
        self.step += 1

    def step0(self):
        far, up, down = (self.a + 2) % 4, (self.a + 1) % 4, (self.a + 3) % 4
        self.c1 = [
            self.send(self.piece(far, 0), self.r1.at[0], self.to(1, 0, 0)),
            self.send(self.piece(far, 1), self.r1.at[1], self.to(3, 0, 0)),
        ]
        self.c2 = [
            self.send(self.piece(up, 1), self.r2.at[0, 1], self.to(1, 0, 0)),
            self.send(self.piece(down, 0), self.r2.at[1, 0], self.to(3, 0, 0)),
        ]

    def step1(self):
        for way, near in ((0, (self.a + 1) % 4), (1, (self.a + 3) % 4)):
            self.c1[way].wait_recv()
            self.add(lambda b: self.index(near, way, b), lambda b: [(self.r1, (way, b))])
            self.c2.append(self.send(self.piece(near, way), self.r2.at[way, way], self.to((1, 3)[way], 0, 0)))

    def step2(self):
        for copy in self.c2:
            copy.wait_recv()
        for z in range(2):
            self.add(lambda b: self.index(self.a, z, b), lambda b: [(self.r2, (way, z, b)) for way in range(2)])
        self.c3 = []
        for dz, db in ((1, 2), (1, 1), (1, 3), (0, 2), (1, 0), (0, 1), (0, 3)):
            target = self.owner_b((self.b + db) % 4)
            src = self.grad.at[self.index(self.a, (self.z + dz) % 2, target)]
            self.c3.append(self.send(src, self.r3.at[dz * 4 + db - 1], self.to(0, dz, db)))

    def step3(self):
        for copy in self.c3:
            copy.wait_recv()
        for part in range(self.grad.shape[3] // 16):
            rows = pl.ds(part * 16, 16)
            total = self.grad[self.index(self.a, self.z, self.owner_b(self.b)) + (rows,)].astype(f32)
            for k in range(7):
                total = total + self.r3[k, rows].astype(f32)
            self.finish(part, total)

    def drain(self):
        for copy in self.sent:
            copy.wait_send()


def layer_kernel(n_copies, names, *refs):
    r = types.SimpleNamespace(**dict(zip(names, refs)))
    side, batch, core = lax.axis_index("side"), lax.axis_index("batch"), lax.axis_index("mp")
    y, z, x = batch // 8, (batch // 4) % 2, batch % 4

    def device(dy, dz, dx):
        return (side, ((y + dy) % 4) * 8 + ((z + dz) % 2) * 4 + (x + dx) % 4, core)

    def across(dx):
        return (1 - side, y * 8 + z * 4 + (x + dx) % 4, core)

    mate = (side, batch, 1 - core)
    count = Counter()
    local = Counter()
    open_sends = []

    def rc(src, dst, to):
        k = count.take()
        return pltpu.make_async_remote_copy(
            src_ref=src, dst_ref=dst, send_sem=r.send.at[k], recv_sem=r.recv.at[k], device_id=to, device_id_type=MESH
        )

    def to_mate(src, dst):
        copy = rc(src, dst, mate)
        copy.start()
        open_sends.append(copy)
        return copy

    def fetch(src, dst):
        copy = pltpu.make_async_copy(src, dst, r.lsem.at[local.take()])
        copy.start()
        return copy

    hid, wqkv, wout, wup, wdown, qkv = r.hid, r.wqkv, r.wout, r.wup, r.wdown, r.qkv
    own_rows = pl.ds(pl.multiple_of(core * ROWS, ROWS), ROWS)

    barrier = pltpu.get_barrier_semaphore()
    steps = [(dy, dz, 0) for dy in range(4) for dz in range(2)] + [(0, dz, dx) for dz in range(2) for dx in (1, 2, 3)]
    greeted = [mate] + [device(*step) for step in steps[1:]] + [across(dx) for dx in range(4)]
    for to in greeted:
        pl.semaphore_signal(barrier, inc=1, device_id=to, device_id_type=MESH)
    got_hid = fetch(r.hidden_in.at[own_rows], hid)
    got_qkv = [fetch(r.w_qkv.at[p], wqkv.at[p, :, pl.ds(0, HALF)]) for p in range(3)]
    got_out = fetch(r.w_out, wout.at[pl.ds(0, HALF)])
    got_up = fetch(r.w_up, wup.at[0])
    got_down = fetch(r.w_down, wdown.at[0])
    got_grad = fetch(r.out_grad.at[core], r.stage)
    pl.semaphore_wait(barrier, len(greeted))

    new_qkv = [to_mate(r.w_qkv.at[p], wqkv.at[p, :, pl.ds(HALF, HALF)]) for p in range(3)]
    new_bias = to_mate(r.bias, r.bias_mate)
    new_out = to_mate(r.w_out, wout.at[pl.ds(HALF, HALF)])
    new_up = to_mate(r.w_up, wup.at[1])
    new_down = to_mate(r.w_down, wdown.at[1])

    mask = r.mask
    for slot in range(SLOTS):
        count_live = r.lengths[core * SLOTS + slot]
        live = iota((SLOT, 256), 0) < count_live
        seen = ((iota((SLOT, 256), 1) // SLOT) == (slot % 4)) | (iota((SLOT, 256), 1) < 256 * side)
        mask[pl.ds(slot * SLOT, SLOT), :] = jnp.where(live & seen, 0.0, -1000000000.0).astype(bf16)

    got_hid.wait()
    new_bias.wait_recv()

    def bias_of(start, width):
        return jnp.concatenate([r.bias[:, start : start + width], r.bias_mate[:, start : start + width]], axis=1)

    for p in range(3):
        got_qkv[p].wait()
        new_qkv[p].wait_recv()
        value = nn(hid[...], wqkv[p])
        if p == 0:
            value = (value + bias_of(1536, HALF)).astype(bf16) * jnp.asarray(0.125, bf16)
        if p == 2:
            value = value + bias_of(1920, HALF)
        qkv[p] = value.astype(bf16)

    ctx, weights = r.ctx, r.weights

    def attend(pair, carry):
        cols = pl.ds(pl.multiple_of(pair * 128, 128), 128)
        for tile in range(3):
            rows = pl.ds(tile * 256, 256)
            scores = nt(split_pair(qkv[1, rows, cols]), qkv[0, rows, cols])
            parts = []
            for h in range(2):
                s = scores[h * 256 : (h + 1) * 256] + mask[rows, :].astype(f32)
                e = jnp.exp(s - jnp.max(s, axis=0, keepdims=True))
                parts.append((e * (1.0 / jnp.sum(e, axis=0, keepdims=True))).astype(bf16))
            w = jnp.concatenate(parts, axis=0)
            weights[pair * 3 + tile] = w
            ctx[rows, cols] = tn(w, split_pair(qkv[2, rows, cols])).astype(bf16)
        return carry

    lax.fori_loop(0, PAIRS, attend, 0)

    cls, line, landed, back, sgrad = r.cls, r.line, r.landed, r.back, r.sgrad
    r.cls_in[...] = jnp.zeros_like(r.cls_in)
    for slot in range(SLOTS):
        rows = pl.ds(slot * SLOT, 16)
        r.cls_in[0, slot : slot + 1, :] = ctx[rows, :].astype(f32)[0:1]
        r.cls_in[1, slot : slot + 1, :] = hid[rows, :].astype(f32)[0:1]
    got_out.wait()
    new_out.wait_recv()
    v = nn(r.cls_in[0].astype(bf16), wout[...]) + r.cls_in[1] + r.b_out[...]
    v = v - mean_of(v)
    v = v * lax.rsqrt(mean_of(v * v) + EPS) * r.ln1_gain[...] + r.ln1_bias[...]
    r.cls_low[...] = v.astype(bf16)
    cls[...] = v + r.b_down[...]
    got_up.wait()
    got_down.wait()
    new_up.wait_recv()
    new_down.wait_recv()
    r.bias_all[0] = r.bias[...]
    r.bias_all[1] = r.bias_mate[...]

    def feed_cls(j, carry):
        half, part = j // 3, j % 3
        inner = pl.ds(pl.multiple_of(part * 512, 512), 512)
        u = nn(r.cls_low[...], wup[half, :, inner]) + r.bias_all[half, :, inner]
        a = (u * (0.5 + 0.5 * lax.erf(u * 0.7071067811865476))).astype(bf16)
        cls[...] += nn(a, wdown[half, part].reshape(512, WIDTH))
        return carry

    lax.fori_loop(0, 6, feed_cls, 0)
    v = cls[...]
    v = v - mean_of(v)
    v = v * lax.rsqrt(mean_of(v * v) + EPS) * r.ln2_gain[...] + r.ln2_bias[...]
    cls[...] = v.astype(bf16).astype(f32)

    shifts = [(dy, dz) for dy in range(4) for dz in range(2)][1:]
    here = y * 2 + z
    give = [rc(r.mine, line.at[x], across(dx)) for dx in range(4)]
    spread = [rc(line, landed.at[here], device(dy, dz, 0)) for dy, dz in shifts]
    gather = [rc(landed.at[((y + dy) % 4) * 2 + ((z + dz) % 2)], r.terms.at[here], device(dy, dz, 0)) for dy, dz in shifts]
    hand = [rc(back.at[(x + dx) % 4], line.at[x], across(dx)) for dx in range(4)]
    swap_p = rc(r.given.at[0], r.given.at[1], mate)
    swap_q = rc(r.ques.at[0], r.ques.at[1], mate)
    send_loss = rc(r.loss, r.loss, across(0))
    sgrad[...] = jnp.zeros_like(sgrad)

    @pl.when(side == 1)
    def _():
        for t in range(3):
            r.mine[pl.ds(t, 1), :] = cls[pl.ds(t * 4, 1), :]
        r.mine[pl.ds(3, 1), :] = cls[pl.ds(0, 1), :]
        for copy in give:
            copy.start()

    @pl.when(side == 0)
    def _():
        r.ques[0] = cls[...].astype(bf16)
        swap_q.start()

    def loss_spread():
        for copy in give:
            copy.wait_recv()
        for copy in spread:
            copy.start()
        landed[here] = line[...]

    def loss_swap():
        for copy in spread:
            copy.wait_recv()
        r.given[0] = landed[...].reshape(128, WIDTH).astype(bf16)
        swap_p.start()

    def loss_values():
        swap_q.wait_recv()
        place = iota((32, 32), 0)
        home = (place // SLOTS) ^ core
        wanted = home * 16 + place % SLOTS
        picks = ((iota((32, 32), 1) == wanted) & (place < 24)).astype(bf16)
        questions = nn(picks, r.ques[...].reshape(32, WIDTH))[0:24]
        swap_p.wait_recv()
        col = iota((192, 256), 0)
        chip, inner = col // 6, col % 6
        owner = inner // 3
        spot = (owner ^ core) * 128 + chip * 4 + inner % 3
        picks = (iota((192, 256), 1) == spot).astype(bf16)
        passages = nn(picks, r.given[...].reshape(256, WIDTH))
        sims = nt(questions.astype(bf16), passages.astype(bf16)) * SIM_SCALE
        chosen = r.positives[...] > 0
        top = jnp.max(sims, axis=1, keepdims=True)
        lse_all = top + jnp.log(jnp.sum(jnp.exp(sims - top), axis=1, keepdims=True))
        picked = jnp.where(chosen, sims, -1000000000.0)
        top_pos = jnp.max(picked, axis=1, keepdims=True)
        lse_pos = top_pos + jnp.log(jnp.sum(jnp.exp(picked - top_pos), axis=1, keepdims=True))
        r.loss[...] = jnp.broadcast_to(lse_all - lse_pos, (24, 128))
        send_loss.start()
        gap = jnp.exp(sims - lse_all) - jnp.where(chosen, jnp.exp(picked - lse_pos), 0.0)
        gap = gap * SIM_SCALE
        col = iota((192, 128), 1)
        source = (col // 4) * 6 + core * 3 + col % 4
        picks = ((iota((192, 128), 0) == source) & (col % 4 < 3)).astype(f32)
        gap_own = nn(gap, picks, HIGH)
        for copy in spread:
            copy.wait_send()
        landed[...] = tn(gap_own, questions, HIGH).reshape(8, 4, 4, WIDTH)
        for copy in gather:
            copy.start()
        sgrad[...] = nn(gap, passages, HIGH)
        r.terms[here] = landed[here]

    def loss_hand():
        for copy in gather:
            copy.wait_recv()
        back[...] = jnp.sum(r.terms[...], axis=0)
        for copy in hand:
            copy.start()

    def loss_back():
        @pl.when(side == 1)
        def _():
            for copy in hand:
                copy.wait_recv()
            summed = jnp.sum(line[...], axis=0)
            for t in range(3):
                sgrad[pl.ds(core * SLOTS + t * 4, 1), :] = summed[t : t + 1]
            send_loss.wait_recv()
            for copy in give:
                copy.wait_send()

        @pl.when(side == 0)
        def _():
            for copy in gather + hand + [swap_p, swap_q, send_loss]:
                copy.wait_send()

        r.losses[...] = r.loss[...]

    n1, roots, low1, f = r.n1, r.roots, r.low1, r.f
    f[...] = nn(ctx[...], wout[...])

    def first_norm(slot, carry):
        rows = pl.ds(pl.multiple_of(slot * SLOT, SLOT), SLOT)
        v = f[rows, :] + hid[rows, :].astype(f32) + r.b_out[...]
        v = v - mean_of(v)
        root = lax.rsqrt(mean_of(v * v) + EPS)
        n = v * root
        n1[rows, :] = n.astype(bf16)
        roots[rows, 0:1] = root
        h1 = n * r.ln1_gain[...] + r.ln1_bias[...]
        low1[rows, :] = h1.astype(bf16)
        f[rows, :] = h1 + r.b_down[...]
        return carry

    lax.fori_loop(0, SLOTS, first_norm, 0)

    act, slope = r.act, r.slope
    pl.when(side == 0)(loss_spread)

    def feed(j, carry):
        half, block = j // 3, j % 3
        pl.when((side == 0) & (j == 2))(loss_swap)
        pl.when((side == 0) & (j == 4))(loss_values)
        inner = pl.ds(pl.multiple_of(block * 512, 512), 512)
        cols = pl.ds(pl.multiple_of(j * 512, 512), 512)
        u = nn(low1[...], wup[half, :, inner]) + r.bias_all[half, :, inner]
        for part in range(6):
            rows = pl.ds(part * 128, 128)
            v = u[part * 128 : (part + 1) * 128]
            cdf = 0.5 + 0.5 * lax.erf(v * 0.7071067811865476)
            bell = jnp.exp(v * v * -0.5) * 0.3989422804014327
            act[rows, cols] = (v * cdf).astype(bf16)
            slope[rows, cols] = (cdf + v * bell).astype(bf16)
        a = act[:, cols]
        for part in range(3):
            out = pl.ds(part * 256, 256)
            f[:, out] += nn(a, wdown[half, block, :, :, :, :, out].reshape(512, 256))
        return carry

    lax.fori_loop(0, 6, feed, 0)
    pl.when(side == 0)(loss_hand)

    low2 = r.d_low

    def second_norm(slot, carry):
        rows = pl.ds(pl.multiple_of(slot * SLOT, SLOT), SLOT)
        v = f[rows, :]
        v = v - mean_of(v)
        root = lax.rsqrt(mean_of(v * v) + EPS)
        n = v * root
        f[rows, :] = n
        roots[rows, 1:2] = root
        e = (n * r.ln2_gain[...] + r.ln2_bias[...]).astype(bf16)
        low2[rows, :] = e
        return carry

    lax.fori_loop(0, SLOTS, second_norm, 0)
    put_encoded = fetch(low2, r.encoded.at[own_rows])
    mate_encoded = to_mate(low2, r.encoded.at[own_rows])

    loss_back()

    d_low, sums, og = r.d_low, r.sums, r.stage
    put_encoded.wait()
    mate_encoded.wait_send()
    open_sends[:] = [copy for copy in open_sends if copy is not mate_encoded]
    got_grad.wait()
    sums[...] = jnp.zeros_like(sums)

    def second_back(block, carry):
        whole = og[block // 2, block % 2].reshape(192, WIDTH)
        for part in range(3):
            slot = block * 3 + part
            rows = pl.ds(pl.multiple_of(slot * SLOT, SLOT), SLOT)
            place = iota((SLOT, WIDTH), 0)
            count_live = r.lengths[core * SLOTS + slot]
            lead = jnp.where((side == 1) & (slot % 4 != 0), 0, 1)
            keep = (place < count_live) & (place >= lead)
            d = jnp.where(keep, whole[part * SLOT : (part + 1) * SLOT].astype(f32), 0.0)
            d = d + jnp.where(place == 0, sgrad[pl.ds(core * SLOTS + slot, 1), :], 0.0)
            n = f[rows, :]
            sums[0] += partial_sum(d * n)
            sums[1] += partial_sum(d)
            d = norm_back(d, n, r.ln2_gain[...], roots[rows, 1:2])
            sums[2] += partial_sum(d)
            f[rows, :] = d
            d_low[rows, :] = d.astype(bf16)
        return carry

    lax.fori_loop(0, 4, second_back, 0)

    where = (x, y, z, device)
    stage = r.stage
    bundles = []

    def start(name, grad, first, finish):
        got = [getattr(r, part + name) for part in ("r1_", "r2_", "r3_")]
        b = Bundle(rc, where, first, grad, *got, finish)
        bundles.append(b)
        b.advance()
        return b

    def columns(ref, first):
        return ref.at[:, :, :, :, pl.ds(first, HALF)]

    def send_half(name, blocks, make, slot):
        grad = getattr(r, "g_" + name)
        per = 4 // blocks
        moves = []
        for k in range(blocks):
            value = make(1, k).astype(bf16)
            if k > 0:
                moves[k - 1].wait_send()
            slot[...] = value
            moves.append(rc(slot, grad.at[pl.ds(k * per, per)], mate))
            moves[k].start()
        return moves

    def keep_half(name, make, moves):
        grad = getattr(r, "g_" + name)
        per = 4 // len(moves)
        for k, move in enumerate(moves):
            span = pl.ds(k * per, per)
            value = make(0, k)
            move.wait_recv()
            grad[span] = (value + grad[span].astype(f32)).astype(bf16)
        moves[-1].wait_send()

    def make_down(half, k):
        cols = pl.ds(half * 1536 + k * 768, 768)
        return tn(act[:, cols], d_low[...]).reshape(2, 2, 4, 48, WIDTH)

    def end_down(first):
        def finish(part, total):
            r.g_w_down[pl.ds(part * 16, 16), pl.ds(first, HALF)] = total

        return finish

    keep_half("down", make_down, send_half("down", 2, make_down, stage))
    down = [
        start("downa", columns(r.g_down, 0), "x", end_down(0)),
        start("downb", columns(r.g_down, HALF), "y", end_down(HALF)),
    ]

    def feed_back(j, carry):
        half, part = j // 3, j % 3
        inner = pl.ds(pl.multiple_of(part * 512, 512), 512)
        cols = pl.ds(pl.multiple_of(j * 512, 512), 512)
        value = nt(d_low[...], wdown[half, part].reshape(512, WIDTH))
        total = jnp.zeros((1, 512), f32)
        for part in range(6):
            rows = pl.ds(part * 128, 128)
            d = (value[part * 128 : (part + 1) * 128] * slope[rows, cols].astype(f32)).astype(bf16)
            slope[rows, cols] = d
            total = total + column_sum(d.astype(f32))
        r.sum_up[:, cols] = total
        d = slope[:, cols]
        for part in range(3):
            out = pl.ds(part * 256, 256)
            f[:, out] += nt(d, wup[half, out, inner])
        return carry

    lax.fori_loop(0, 4, feed_back, 0)
    for b in down:
        b.advance()
    lax.fori_loop(4, 6, feed_back, 0)
    pl.semaphore_signal(r.free, inc=1, device_id=mate, device_id_type=MESH)

    def make_up(half, k):
        value = tn(low1[:, pl.ds(k * 384, 384)], slope[:, pl.ds(half * 1536, 1536)])
        left = value[:, :768].reshape(48, 8, WIDTH)
        right = value[:, 768:].reshape(48, 8, WIDTH)
        return jnp.concatenate([left, right], axis=1).reshape(2, 2, 4, 48, WIDTH)

    def end_up(first):
        def finish(part, total):
            rows = pl.ds(part * 8, 8)
            r.g_w_up[rows, pl.ds(first, HALF)] = total[:8]
            r.g_w_up[rows, pl.ds(768 + first, HALF)] = total[8:]

        return finish

    keep_half("up", make_up, send_half("up", 2, make_up, stage))
    up = [
        start("upa", columns(r.g_up, 0), "x", end_up(0)),
        start("upb", columns(r.g_up, HALF), "y", end_up(HALF)),
    ]

    def first_back(slot, carry):
        rows = pl.ds(pl.multiple_of(slot * SLOT, SLOT), SLOT)
        d = f[rows, :]
        n = n1[rows, :].astype(f32)
        sums[3] += partial_sum(d * n)
        sums[4] += partial_sum(d)
        d = norm_back(d, n, r.ln1_gain[...], roots[rows, 0:1])
        sums[5] += partial_sum(d)
        f[rows, :] = d
        d_low[rows, :] = d.astype(bf16)
        return carry

    lax.fori_loop(0, SLOTS, first_back, 0)
    for b in down:
        b.advance()

    def make_out(half, k):
        value = tn(ctx[:, pl.ds(half * HALF, HALF)], d_low[...])
        left = value[:, :HALF].reshape(48, 8, HALF)
        right = value[:, HALF:].reshape(48, 8, HALF)
        return jnp.concatenate([left, right], axis=1).reshape(4, 2, 2, 48, HALF)

    def end_out(part, total):
        rows = pl.ds(part * 8, 8)
        r.g_w_out[rows, pl.ds(0, HALF)] = total[:8]
        r.g_w_out[rows, pl.ds(HALF, HALF)] = total[8:]

    moves = send_half("out", 1, make_out, r.stage_out)
    act[:, 0:WIDTH] = nt(d_low[...], wout[...]).astype(bf16)
    keep_half("out", make_out, moves)
    out = start("out", r.g_out, "y", end_out)

    def pair_back(pair):
        cols = pl.ds(pl.multiple_of(pair * 128, 128), 128)

        for tile in range(3):
            rows = pl.ds(tile * 256, 256)
            q, k, d = qkv[0, rows, cols], qkv[1, rows, cols], act[rows, cols]
            w = weights[pair * 3 + tile]
            dw = nt(split_pair(qkv[2, rows, cols]), d)
            parts = []
            for h in range(2):
                wh = w[h * 256 : (h + 1) * 256].astype(f32)
                dh = dw[h * 256 : (h + 1) * 256]
                parts.append((wh * (dh - column_sum(wh * dh))).astype(bf16))
            ds = jnp.concatenate(parts, axis=0)
            qkv[0, rows, cols] = (tn(ds, split_pair(k)) * 0.125).astype(bf16)
            qkv[1, rows, cols] = merge_pair(nn(ds, q)).astype(bf16)
            qkv[2, rows, cols] = merge_pair(nn(w, d)).astype(bf16)
        sums[6, :, cols] = partial_sum(qkv[0, :, cols].astype(f32))
        sums[7, :, cols] = partial_sum(qkv[2, :, cols].astype(f32))

    def make_qkv(pair):
        cols = pl.ds(pair * 128, 128)
        d = jnp.concatenate([qkv[p, :, cols] for p in range(3)], axis=1)
        value = tn(hid[...], d).reshape(32, 24, HALF)
        a, b, c = value[:, 0:8], value[:, 8:16], value[:, 16:24]
        top = jnp.concatenate([a, b[:, :, :256]], axis=2)
        low = jnp.concatenate([b[:, :, 256:], c, jnp.zeros((32, 8, 128), f32)], axis=2)
        return jnp.concatenate([top, low], axis=1).reshape(4, 2, 4, 16, 640)

    def end_qkv(pair, first):
        def finish(part, total):
            r.sum_qkv[pair, :, pl.ds(first, total.shape[1])] = total

        return finish

    grad_qkv = [wdown.at[1, k, :, :, :, :, pl.ds(0, 640)] for k in range(3)]
    stage_qkv = [wdown.at[0, k, :, :, :, :, pl.ds(0, 640)] for k in range(3)]
    moves_qkv = [rc(stage_qkv[k], grad_qkv[k], mate) for k in range(3)]
    pl.semaphore_wait(r.free, 1)
    for k in range(3):
        pair_back(3 + k)
        stage_qkv[k][...] = make_qkv(3 + k).astype(bf16)
        moves_qkv[k].start()
        for b in (up, down + [out], [])[k]:
            b.advance()
    last = []
    for k in range(3):
        pair_back(k)
        value = make_qkv(k)
        moves_qkv[k].wait_recv()
        grad_qkv[k][...] = (value + grad_qkv[k][...].astype(f32)).astype(bf16)
        for part, first, start_col, width in (("a", "x", 0, HALF), ("b", "y", HALF, 256)):
            view = wdown.at[1, k, :, :, :, :, pl.ds(start_col, width)]
            last.append(start("qkv%d" % k + part, view, first, end_qkv(k, start_col)))
        if k == 1:
            for b in up + [out]:
                b.advance()
    for k in range(3):
        moves_qkv[k].wait_send()

    vec = r.vec

    def pack(half):
        up = r.sum_up[:, pl.ds(half * 1536, 1536)]
        cols = pl.ds(half * HALF, HALF)
        qv = jnp.concatenate([column_sum(sums[6, :, cols]), column_sum(sums[7, :, cols])], axis=1)
        common = [column_sum(sums[k]) for k in range(6)]
        return jnp.concatenate([up[:, :768], up[:, 768:], qv] + common + [jnp.zeros((7, WIDTH), f32)], axis=0)

    vec[0] = pack(1)
    vec[1] = pack(0)
    vec_mate = to_mate(vec.at[0], vec.at[2])
    vec_state = {}

    def vec_go(buffer, place, ways):
        copies = []
        for way in ways:
            copy = rc(buffer.at[place], buffer.at[place], device(*way))
            copy.start()
            open_sends.append(copy)
            copies.append(copy)
        vec_state["open"] = copies

    def vec_wait():
        for copy in vec_state["open"]:
            copy.wait_recv()

    f[...] += nt(qkv[0], wqkv[0])
    vec_mate.wait_recv()
    r.vec_x[x] = vec[1] + vec[2]
    vec_go(r.vec_x, x, [(0, 0, dx) for dx in (1, 2, 3)])
    for b in last[0:4]:
        b.advance()
    f[...] += nt(qkv[1], wqkv[1])
    for b in [out]:
        b.advance()
    ctx[...] = (f[...] + nt(qkv[2], wqkv[2])).astype(bf16)
    put_grad = fetch(ctx, r.input_grad.at[own_rows])
    mate_grad = to_mate(ctx, r.input_grad.at[own_rows])
    vec_wait()
    r.vec_y[y] = jnp.sum(r.vec_x[...], axis=0)
    vec_go(r.vec_y, y, [(dy, 0, 0) for dy in (1, 2, 3)])
    for b in last[4:6] + up + last[0:4]:
        b.advance()
    vec_wait()
    r.vec_z[z] = jnp.sum(r.vec_y[...], axis=0)
    vec_go(r.vec_z, z, [(0, 1, 0)])
    for b in last[4:6] + last[0:4] + last[4:6]:
        b.advance()
    vec_wait()
    r.g_vec[...] = r.vec_z[0] + r.vec_z[1]
    for k in range(3):
        t = r.sum_qkv[k]
        top, low = t[:8], t[8:]
        whole = jnp.concatenate(
            [top[:, :HALF], jnp.concatenate([top[:, HALF:], low[:, :128]], axis=1), low[:, 128:512]], axis=0
        )
        for p in range(3):
            r.g_w_qkv[p, :, pl.ds(k * 128, 128)] = whole[:, p * 128 : (p + 1) * 128]
    put_grad.wait()
    mate_grad.wait_recv()
    mate_encoded.wait_recv()
    for copy in open_sends:
        copy.wait_send()
    assert all(b.step == 4 for b in bundles)
    for b in bundles:
        b.drain()
    assert count.n <= n_copies, count.n


N_COPIES = 208


def layer(lengths, far_in, near_in):
    in_names = ["lengths"] + list(far_in) + list(near_in)
    vmem, far = pl.BlockSpec(memory_space=pltpu.VMEM), pl.BlockSpec(memory_space=pl.ANY)
    in_specs = [pl.BlockSpec(memory_space=pltpu.SMEM)] + [far] * len(far_in) + [vmem] * len(near_in)
    outs = dict(
        encoded=((1536, WIDTH), bf16, far),
        input_grad=((1536, WIDTH), bf16, far),
        losses=((24, 128), f32, vmem),
        g_w_qkv=((3, 24, HALF), f32, vmem),
        g_w_out=((24, WIDTH), f32, vmem),
        g_w_up=((24, 1536), f32, vmem),
        g_w_down=((48, WIDTH), f32, vmem),
        g_vec=((16, WIDTH), f32, vmem),
    )
    scratch = dict(
        hid=((ROWS, WIDTH), bf16),
        wqkv=((3, WIDTH, WIDTH), bf16),
        wout=((WIDTH, WIDTH), bf16),
        wup=((2, WIDTH, 1536), bf16),
        wdown=((2, 3, 4, 2, 4, 16, WIDTH), bf16),
        qkv=((3, ROWS, WIDTH), bf16),
        weights=((18, 512, 256), bf16),
        ctx=((ROWS, WIDTH), bf16),
        n1=((ROWS, WIDTH), bf16),
        low1=((ROWS, WIDTH), bf16),
        act=((ROWS, 3072), bf16),
        slope=((ROWS, 3072), bf16),
        f=((ROWS, WIDTH), f32),
        d_low=((ROWS, WIDTH), bf16),
        roots=((ROWS, 2), f32),
        mask=((ROWS, 256), bf16),
        bias_mate=((1, 2304), f32),
        bias_all=((2, 1, 2304), f32),
        cls=((16, WIDTH), f32),
        mine=((4, WIDTH), f32),
        cls_in=((2, 16, WIDTH), f32),
        cls_low=((16, WIDTH), bf16),
        line=((4, 4, WIDTH), f32),
        back=((4, 4, WIDTH), f32),
        landed=((8, 4, 4, WIDTH), f32),
        terms=((8, 4, 4, WIDTH), f32),
        sum_qkv=((3, 16, 640), f32),
        g_down=((4, 2, 4, 48, WIDTH), bf16),
        g_up=((4, 2, 4, 48, WIDTH), bf16),
        g_out=((4, 2, 2, 48, HALF), bf16),
        given=((2, 128, WIDTH), bf16),
        ques=((2, 16, WIDTH), bf16),
        loss=((24, 128), f32),
        sgrad=((24, WIDTH), f32),
        sums=((8, 8, WIDTH), f32),
        sum_up=((1, 3072), f32),
        stage=((2, 2, 4, 48, WIDTH), bf16),
        stage_out=((4, 2, 2, 48, HALF), bf16),
        vec=((3, 16, WIDTH), f32),
        vec_x=((4, 16, WIDTH), f32),
        vec_y=((4, 16, WIDTH), f32),
        vec_z=((2, 16, WIDTH), f32),
    )

    def buffers(name, last, rows, cols):
        scratch["r1_" + name] = ((2, last, rows, cols), bf16)
        scratch["r2_" + name] = ((2, 2, last, rows, cols), bf16)
        scratch["r3_" + name] = ((7, rows, cols), bf16)

    for part in "ab":
        buffers("down" + part, 4, 48, HALF)
        buffers("up" + part, 4, 48, HALF)
        for k in range(3):
            buffers("qkv%d" % k + part, 4, 16, HALF if part == "a" else 256)
    buffers("out", 2, 48, HALF)
    sems = dict(
        send=pltpu.SemaphoreType.DMA((N_COPIES,)),
        recv=pltpu.SemaphoreType.DMA((N_COPIES,)),
        lsem=pltpu.SemaphoreType.DMA((16,)),
        free=pltpu.SemaphoreType.REGULAR,
    )
    names = in_names + list(outs) + list(scratch) + list(sems)
    results = pl.pallas_call(
        functools.partial(layer_kernel, N_COPIES, names),
        name="layer",
        out_shape=[jax.ShapeDtypeStruct(shape, kind) for shape, kind, _ in outs.values()],
        in_specs=in_specs,
        out_specs=[spec for _, _, spec in outs.values()],
        scratch_shapes=[pltpu.VMEM(shape, kind) for shape, kind in scratch.values()] + list(sems.values()),
        compiler_params=pltpu.CompilerParams(
            collective_id=0, has_side_effects=True, vmem_limit_bytes=VMEM_LIMIT
        ),
    )(lengths, *far_in.values(), *near_in.values())
    return types.SimpleNamespace(**dict(zip(outs, results)))


VMEM_LIMIT = 64 * 1024 * 1024 - 256 * 1024


def finish_kernel(copies, names, *refs):
    r = types.SimpleNamespace(**dict(zip(names, refs)))
    batch = lax.axis_index("batch")
    moves = []
    for name in copies:
        src, hold, dst = getattr(r, name), getattr(r, "hold_" + name), getattr(r, "out_" + name)
        parts = 4 if src.shape[0] == 1536 else 1
        rows = src.shape[0] // parts
        for part in range(parts):
            span, k = pl.ds(part * rows, rows), len(moves)
            first = pltpu.make_async_copy(src.at[span], hold.at[span], r.sems.at[0, k])
            first.start()
            moves.append((first, pltpu.make_async_copy(hold.at[span], dst.at[span], r.sems.at[1, k])))
    common = pltpu.roll(r.vec[...], (WIDTH - batch * 24) % WIDTH, 1)
    for k, ref in enumerate((r.ln2_gain, r.ln2_bias, r.b_down, r.ln1_gain, r.ln1_bias, r.b_out)):
        ref[...] = common[3 + k : 4 + k, 0:24]
    up = pltpu.roll(r.vec[...], (WIDTH - (batch % 16) * 48) % WIDTH, 1)
    r.b_up[...] = jnp.where(batch < 16, up[0:1, 0:48], up[1:2, 0:48])
    qv = pltpu.roll(r.vec[...], (WIDTH - batch * 12) % WIDTH, 1)
    r.b_qv[0:1, :] = qv[2:3, 0:12]
    r.b_qv[1:2, :] = qv[2:3, HALF : HALF + 12]
    for k in range(12):
        r.out_w_out[k] = r.w_out[pl.ds((batch % 2) * 12 + k, 1), :]
    diagonal = iota((24, 128), 0) == iota((24, 128), 1)
    r.loss[...] = column_sum(jnp.where(diagonal, r.losses[...], 0.0))[:, 0:24]
    for first, second in moves:
        first.wait()
        second.start()
    for _, second in moves:
        second.wait()


def finish(out):
    far, vmem = pl.BlockSpec(memory_space=pl.ANY), pl.BlockSpec(memory_space=pltpu.VMEM)
    large = dict(encoded=out.encoded, input_grad=out.input_grad, w_qkv=out.g_w_qkv, w_up=out.g_w_up, w_down=out.g_w_down)
    small = dict(w_out=out.g_w_out, vec=out.g_vec, losses=out.losses)
    row = jax.ShapeDtypeStruct((1, 24), f32)
    results = dict(
        out_w_out=jax.ShapeDtypeStruct((12, 1, WIDTH), f32),
        b_qv=jax.ShapeDtypeStruct((2, 12), f32),
        b_up=jax.ShapeDtypeStruct((1, 48), f32),
        b_down=row,
        b_out=row,
        ln1_gain=row,
        ln1_bias=row,
        ln2_gain=row,
        ln2_bias=row,
        loss=row,
    )
    moved = {"out_" + name: jax.ShapeDtypeStruct(value.shape, value.dtype) for name, value in large.items()}
    names = list(large) + list(small) + list(moved) + list(results) + ["hold_" + name for name in large] + ["sems"]
    values = pl.pallas_call(
        functools.partial(finish_kernel, list(large), names),
        name="finish",
        out_shape=list(moved.values()) + list(results.values()),
        in_specs=[far] * len(large) + [vmem] * len(small),
        out_specs=[far] * len(moved) + [vmem] * len(results),
        scratch_shapes=[pltpu.VMEM(value.shape, value.dtype) for value in large.values()] + [pltpu.SemaphoreType.DMA((2, 16))],
        compiler_params=pltpu.CompilerParams(vmem_limit_bytes=VMEM_LIMIT),
    )(*large.values(), *small.values())
    return types.SimpleNamespace(**dict(zip(list(moved) + list(results), values)))


def on_device(
    hidden_in, w_qkv, b_qv, w_out, b_out, ln1_gain, ln1_bias, w_up, b_up, w_down, b_down, ln2_gain, ln2_bias, lengths, positives, out_grad
):
    out = layer(
        lengths[0],
        dict(
            hidden_in=hidden_in[0],
            w_qkv=jnp.transpose(w_qkv[0], (1, 0, 2)),
            w_out=w_out[0],
            w_up=w_up[0],
            w_down=w_down[0].reshape(3, 4, 2, 4, 16, WIDTH),
            out_grad=out_grad[0].reshape(2, 2, 2, 4, 48, WIDTH),
        ),
        dict(
            bias=jnp.concatenate([b_up[0], b_qv[0, 0], b_qv[0, 1]])[None],
            b_out=b_out,
            ln1_gain=ln1_gain,
            ln1_bias=ln1_bias,
            b_down=b_down,
            ln2_gain=ln2_gain,
            ln2_bias=ln2_bias,
            positives=positives,
        ),
    )
    out = finish(out)
    return (
        out.out_encoded[None],
        out.out_input_grad[None],
        out.loss[0],
        jnp.transpose(out.out_w_qkv, (1, 0, 2))[None],
        out.b_qv[None],
        jnp.transpose(out.out_w_out, (1, 0, 2)),
        out.b_out,
        out.ln1_gain,
        out.ln1_bias,
        out.out_w_up[None],
        out.b_up,
        out.out_w_down[None],
        out.b_down,
        out.ln2_gain,
        out.ln2_bias,
    )


def solution(mesh):
    placed = (
        P("side", "batch", None),
        P("side", None, None, "mp"),
        P("side", None, "mp"),
        P("side", "mp", None),
        P("side", None),
        P("side", None),
        P("side", None),
        P("side", None, "mp"),
        P("side", "mp"),
        P("side", "mp", None),
        P("side", None),
        P("side", None),
        P("side", None),
        P("side", "batch"),
        P("batch", None),
        P("side", "batch", None),
    )
    return jax.shard_map(
        on_device,
        mesh=mesh,
        in_specs=placed,
        out_specs=(
            P("side", "batch", None),
            P("side", "batch", None),
            P("batch"),
            P("side", "batch", None, "mp"),
            P("side", None, ("mp", "batch")),
            P("side", ("mp", "batch"), None),
            P("side", "batch"),
            P("side", "batch"),
            P("side", "batch"),
            P("side", "batch", "mp"),
            P("side", ("mp", "batch")),
            P("side", ("mp", "batch"), None),
            P("side", "batch"),
            P("side", "batch"),
            P("side", "batch"),
        ),
        check_vma=False,
    )
```

```python
import functools
import types

import jax
import jax.numpy as jnp
from jax import lax
from jax.experimental import pallas as pl
from jax.experimental.pallas import tpu as pltpu
from jax.sharding import PartitionSpec as P

MESH = pl.DeviceIdType.MESH
bf16 = jnp.bfloat16
f32 = jnp.float32
WIDTH = 768
HALF = 384
ROWS = 768
SLOT = 64
SLOTS = 12
PAIRS = 6
EPS = 1e-05
SIM_SCALE = 0.1
HIGH = lax.Precision.HIGHEST


def nn(a, b, precision=None):
    return lax.dot_general(a, b, (((1,), (0,)), ((), ())), precision=precision, preferred_element_type=f32)


def nt(a, b, precision=None):
    return lax.dot_general(a, b, (((1,), (1,)), ((), ())), precision=precision, preferred_element_type=f32)


def tn(a, b, precision=None):
    return lax.dot_general(a, b, (((0,), (0,)), ((), ())), precision=precision, preferred_element_type=f32)


def iota(shape, axis):
    return lax.broadcasted_iota(jnp.int32, shape, axis)


def split_pair(block):
    first = iota(block.shape, 1) < 64
    zero = jnp.zeros_like(block)
    return jnp.concatenate([jnp.where(first, block, zero), jnp.where(first, zero, block)], axis=0)


def merge_pair(stacked):
    rows = stacked.shape[0] // 2
    first = iota((rows, 128), 1) < 64
    return jnp.where(first, stacked[:rows], stacked[rows:])


def mean_of(values):
    return jnp.sum(values, axis=1, keepdims=True) * (1.0 / WIDTH)


def norm_back(d, n, gain, root):
    u = d * gain
    return (u - mean_of(u) - n * mean_of(u * n)) * root


def partial_sum(values):
    return jnp.sum(values.reshape(values.shape[0] // 8, 8, values.shape[1]), axis=0)


def column_sum(values):
    return jnp.sum(values, axis=0, keepdims=True)


class Counter:
    def __init__(self):
        self.n = 0

    def take(self):
        self.n += 1
        return self.n - 1


class Bundle:
    def __init__(self, group, where, first, grad, r1, r2, r3, finish, apart):
        self.first, self.grad, self.finish, self.apart = first, grad, finish, apart
        self.r1, self.r2, self.r3 = r1, r2, r3
        self.x, self.y, self.z, self.device = where
        self.a = self.y if first == "y" else self.x
        self.b = self.x if first == "y" else self.y
        self.last = grad.shape[2] if first == "y" else grad.shape[0]
        self.step = 0
        far = r3.at[pl.ds(0, self.last)], r3.at[pl.ds(4, 3)]
        self.landing = (r1, r2) + (far if apart else (r3,))
        self.group = [group() for _ in self.landing]

    def index(self, a, z, b):
        return (a, z, b) if self.first == "y" else (b, z, a)

    def piece(self, a, z):
        return self.grad.at[a, z] if self.first == "y" else self.grad.at[:, z, a]

    def to(self, da, dz, db):
        return self.device(da, dz, db) if self.first == "y" else self.device(db, dz, da)

    def owner_b(self, b):
        return b if self.last == 4 else b // 2

    def send(self, step, src, dst, to):
        self.group[step](src, dst, to).start()

    def wait(self, step):
        self.group[step](self.landing[step], self.landing[step], self.to(1, 0, 0)).wait_recv()

    def add(self, where, others):
        def step(k, carry):
            totals = []
            for b in (k * 2, k * 2 + 1):
                total = self.grad[where(b)].astype(f32)
                for ref, index in others(b):
                    total = total + ref[index].astype(f32)
                totals.append(total.astype(bf16))
            for b, total in enumerate(totals):
                self.grad[where(k * 2 + b)] = total
            return carry

        lax.fori_loop(0, self.last // 2, step, 0)

    def advance(self):
        if self.apart:
            (self.step0, self.step1, self.step2z, self.step3z, self.step4)[self.step]()
        else:
            (self.step0, self.step1, self.step2, self.step4)[self.step]()
        self.step += 1

    def done(self):
        return self.step == len(self.landing) + 1

    def step0(self):
        far, up, down = (self.a + 2) % 4, (self.a + 1) % 4, (self.a + 3) % 4
        self.send(0, self.piece(far, 0), self.r1.at[0], self.to(1, 0, 0))
        self.send(0, self.piece(far, 1), self.r1.at[1], self.to(3, 0, 0))
        self.send(1, self.piece(up, 1), self.r2.at[0, 1], self.to(1, 0, 0))
        self.send(1, self.piece(down, 0), self.r2.at[1, 0], self.to(3, 0, 0))

    def step1(self):
        self.wait(0)
        for way, near in ((0, (self.a + 1) % 4), (1, (self.a + 3) % 4)):
            self.add(lambda b: self.index(near, way, b), lambda b: [(self.r1, (way, b))])
            self.send(1, self.piece(near, way), self.r2.at[way, way], self.to((1, 3)[way], 0, 0))

    def own_quarter(self, z):
        self.add(lambda b: self.index(self.a, z, b), lambda b: [(self.r2, (way, z, b)) for way in range(2)])

    def step2(self):
        self.wait(1)
        for z in range(2):
            self.own_quarter(z)
        for dz, db in ((1, 2), (1, 1), (1, 3), (0, 2), (1, 0), (0, 1), (0, 3)):
            src = self.grad.at[self.index(self.a, (self.z + dz) % 2, self.owner_b((self.b + db) % 4))]
            self.send(2, src, self.r3.at[dz * 4 + db - 1], self.to(0, dz, db))

    def step2z(self):
        self.wait(1)
        self.own_quarter(1 - self.z)
        self.send(2, self.piece(self.a, 1 - self.z), self.landing[2], self.to(0, 1, 0))
        self.own_quarter(self.z)

    def step3z(self):
        self.wait(2)
        self.add(lambda b: self.index(self.a, self.z, b), lambda b: [(self.r3, (b,))])
        for db in (2, 1, 3):
            src = self.grad.at[self.index(self.a, self.z, self.owner_b((self.b + db) % 4))]
            self.send(3, src, self.r3.at[3 + db], self.to(0, 0, db))

    def step4(self):
        self.wait(len(self.landing) - 1)
        for part in range(self.grad.shape[3] // 16):
            rows = pl.ds(part * 16, 16)
            total = self.grad[self.index(self.a, self.z, self.owner_b(self.b)) + (rows,)].astype(f32)
            for k in range(4, 7) if self.apart else range(7):
                total = total + self.r3[k, rows].astype(f32)
            self.finish(part, total)

    def drain(self):
        for step, landing in enumerate(self.landing):
            self.group[step](landing, landing, self.to(1, 0, 0)).wait_send()


def layer_kernel(n_copies, names, *refs):
    r = types.SimpleNamespace(**dict(zip(names, refs)))
    side, batch, core = lax.axis_index("side"), lax.axis_index("batch"), lax.axis_index("mp")
    y, z, x = batch // 8, (batch // 4) % 2, batch % 4

    def device(dy, dz, dx):
        return (side, ((y + dy) % 4) * 8 + ((z + dz) % 2) * 4 + (x + dx) % 4, core)

    def across(dx):
        return (1 - side, y * 8 + z * 4 + (x + dx) % 4, core)

    mate = (side, batch, 1 - core)
    count = Counter()
    local = Counter()
    open_sends = []

    def rc(src, dst, to):
        k = count.take()
        return pltpu.make_async_remote_copy(
            src_ref=src, dst_ref=dst, send_sem=r.send.at[k], recv_sem=r.recv.at[k], device_id=to, device_id_type=MESH
        )

    def group():
        k = count.take()

        def make(src, dst, to):
            return pltpu.make_async_remote_copy(
                src_ref=src, dst_ref=dst, send_sem=r.send.at[k], recv_sem=r.recv.at[k], device_id=to, device_id_type=MESH
            )

        return make

    def to_mate(src, dst):
        copy = rc(src, dst, mate)
        copy.start()
        open_sends.append(copy)
        return copy

    def fetch(src, dst):
        copy = pltpu.make_async_copy(src, dst, r.lsem.at[local.take()])
        copy.start()
        return copy

    hid, wqkv, wout, wup, wdown, qkv = r.hid, r.wqkv, r.wout, r.wup, r.wdown, r.qkv
    own_rows = pl.ds(pl.multiple_of(core * ROWS, ROWS), ROWS)

    barrier = pltpu.get_barrier_semaphore()
    steps = [(dy, dz, 0) for dy in range(4) for dz in range(2)] + [(0, dz, dx) for dz in range(2) for dx in (1, 2, 3)]
    greeted = [mate] + [device(*step) for step in steps[1:]] + [across(dx) for dx in range(4)]
    for to in greeted:
        pl.semaphore_signal(barrier, inc=1, device_id=to, device_id_type=MESH)
    got_hid = fetch(r.hidden_in.at[own_rows], hid)
    got_qkv = [fetch(r.w_qkv.at[p], wqkv.at[p, :, pl.ds(0, HALF)]) for p in range(3)]

    mask = r.mask
    for slot in range(SLOTS):
        count_live = r.lengths[core * SLOTS + slot]
        live = iota((SLOT, 256), 0) < count_live
        seen = ((iota((SLOT, 256), 1) // SLOT) == (slot % 4)) | (iota((SLOT, 256), 1) < 256 * side)
        mask[pl.ds(slot * SLOT, SLOT), :] = jnp.where(live & seen, 0.0, -1000000000.0).astype(bf16)

    r.bias_qv[0] = r.b_qv[...]
    r.bias_up[0] = r.b_up[...]
    got_hid.wait()

    def project(p, half):
        cols = pl.ds(half * HALF, HALF)
        value = nn(hid[...], wqkv[p, :, cols])
        if p == 0:
            value = (value + r.bias_qv[half, 0:1, :]).astype(bf16) * jnp.asarray(0.125, bf16)
        if p == 2:
            value = value + r.bias_qv[half, 1:2, :]
        qkv[p, :, cols] = value.astype(bf16)

    for p in range(3):
        got_qkv[p].wait()
        project(p, 0)
    pl.semaphore_wait(barrier, len(greeted))
    new_qkv = [to_mate(r.w_qkv.at[p], wqkv.at[p, :, pl.ds(HALF, HALF)]) for p in range(3)]
    new_qv = to_mate(r.b_qv, r.bias_qv.at[1])
    new_bias = to_mate(r.b_up, r.bias_up.at[1])
    got_out = fetch(r.w_out, wout.at[pl.ds(0, HALF)])
    got_up = fetch(r.w_up, wup.at[0])
    got_down = fetch(r.w_down, wdown.at[0])
    got_grad = fetch(r.out_grad.at[core], r.stage)

    ctx, weights = r.ctx, r.weights

    def attend(pair, carry):
        cols = pl.ds(pl.multiple_of(pair * 128, 128), 128)
        for tile in range(3):
            rows = pl.ds(tile * 256, 256)
            scores = nt(split_pair(qkv[1, rows, cols]), qkv[0, rows, cols])
            parts = []
            for h in range(2):
                s = scores[h * 256 : (h + 1) * 256] + mask[rows, :].astype(f32)
                e = jnp.exp(s - jnp.max(s, axis=0, keepdims=True))
                parts.append((e * (1.0 / jnp.sum(e, axis=0, keepdims=True))).astype(bf16))
            w = jnp.concatenate(parts, axis=0)
            weights[pair * 3 + tile] = w
            ctx[rows, cols] = tn(w, split_pair(qkv[2, rows, cols])).astype(bf16)
        return carry

    lax.fori_loop(0, 2, attend, 0)
    for copy in new_qkv:
        copy.wait_send()
    open_sends[:] = [copy for copy in open_sends if not any(copy is other for other in new_qkv)]
    new_out = to_mate(r.w_out, wout.at[pl.ds(HALF, HALF)])
    new_up = to_mate(r.w_up, wup.at[1])
    new_down = to_mate(r.w_down, wdown.at[1])
    lax.fori_loop(2, 3, attend, 0)
    new_qv.wait_recv()
    for p in range(3):
        new_qkv[p].wait_recv()
        project(p, 1)
    lax.fori_loop(3, PAIRS, attend, 0)

    cls, line, landed, back, sgrad = r.cls, r.line, r.landed, r.back, r.sgrad
    r.cls_in[...] = jnp.zeros_like(r.cls_in)
    for slot in range(SLOTS):
        rows = pl.ds(slot * SLOT, 16)
        r.cls_in[0, slot : slot + 1, :] = ctx[rows, :].astype(f32)[0:1]
        r.cls_in[1, slot : slot + 1, :] = hid[rows, :].astype(f32)[0:1]
    got_out.wait()
    new_out.wait_recv()
    v = nn(r.cls_in[0].astype(bf16), wout[...]) + r.cls_in[1] + r.b_out[...]
    v = v - mean_of(v)
    v = v * lax.rsqrt(mean_of(v * v) + EPS) * r.ln1_gain[...] + r.ln1_bias[...]
    r.cls_low[...] = v.astype(bf16)
    cls[...] = v + r.b_down[...]
    got_up.wait()
    got_down.wait()
    new_up.wait_recv()
    new_down.wait_recv()
    new_bias.wait_recv()

    def feed_cls(j, carry):
        half, part = j // 3, j % 3
        inner = pl.ds(pl.multiple_of(part * 512, 512), 512)
        u = nn(r.cls_low[...], wup[half, :, inner]) + r.bias_up[half, :, inner]
        a = (u * (0.5 + 0.5 * lax.erf(u * 0.7071067811865476))).astype(bf16)
        cls[...] += nn(a, wdown[half, part].reshape(512, WIDTH))
        return carry

    lax.fori_loop(0, 6, feed_cls, 0)
    v = cls[...]
    v = v - mean_of(v)
    v = v * lax.rsqrt(mean_of(v * v) + EPS) * r.ln2_gain[...] + r.ln2_bias[...]
    cls[...] = v.astype(bf16).astype(f32)

    shifts = [(dy, dz) for dy in range(4) for dz in range(2)][1:]
    here = y * 2 + z
    give = [rc(r.mine, line.at[x], across(dx)) for dx in range(4)]
    spread = [rc(r.around, landed.at[here], device(dy, dz, 0)) for dy, dz in shifts]
    gather = [rc(landed.at[((y + dy) % 4) * 2 + ((z + dz) % 2)], r.terms.at[here], device(dy, dz, 0)) for dy, dz in shifts]
    hand = [rc(back.at[(x + dx) % 4], line.at[x], across(dx)) for dx in range(4)]
    swap_p = rc(r.given.at[0], r.given.at[1], mate)
    swap_q = rc(r.ques.at[0], r.ques.at[1], mate)
    send_loss = rc(r.loss, r.loss, across(0))
    sgrad[...] = jnp.zeros_like(sgrad)

    @pl.when(side == 1)
    def _():
        for t in range(3):
            r.mine[pl.ds(t, 1), :] = cls[pl.ds(t * 4, 1), :]
        r.mine[pl.ds(3, 1), :] = cls[pl.ds(0, 1), :]
        for copy in give:
            copy.start()

    @pl.when(side == 0)
    def _():
        r.ques[0] = cls[...].astype(bf16)
        swap_q.start()

    def loss_spread():
        for copy in give:
            copy.wait_recv()
        r.around[...] = line[...].reshape(16, WIDTH).astype(bf16)
        for copy in spread:
            copy.start()
        landed[here] = r.around[...]

    def loss_swap():
        for copy in spread:
            copy.wait_recv()
        r.given[0] = landed[...].reshape(128, WIDTH)
        swap_p.start()

    def loss_values():
        swap_q.wait_recv()
        place = iota((32, 32), 0)
        home = (place // SLOTS) ^ core
        wanted = home * 16 + place % SLOTS
        picks = ((iota((32, 32), 1) == wanted) & (place < 24)).astype(bf16)
        questions = nn(picks, r.ques[...].reshape(32, WIDTH))[0:24]
        swap_p.wait_recv()
        col = iota((192, 256), 0)
        chip, inner = col // 6, col % 6
        owner = inner // 3
        spot = (owner ^ core) * 128 + chip * 4 + inner % 3
        picks = (iota((192, 256), 1) == spot).astype(bf16)
        passages = nn(picks, r.given[...].reshape(256, WIDTH))
        sims = nt(questions.astype(bf16), passages.astype(bf16)) * SIM_SCALE
        chosen = r.positives[...] > 0
        top = jnp.max(sims, axis=1, keepdims=True)
        lse_all = top + jnp.log(jnp.sum(jnp.exp(sims - top), axis=1, keepdims=True))
        picked = jnp.where(chosen, sims, -1000000000.0)
        top_pos = jnp.max(picked, axis=1, keepdims=True)
        lse_pos = top_pos + jnp.log(jnp.sum(jnp.exp(picked - top_pos), axis=1, keepdims=True))
        r.loss[...] = jnp.broadcast_to(lse_all - lse_pos, (24, 128))
        send_loss.start()
        gap = jnp.exp(sims - lse_all) - jnp.where(chosen, jnp.exp(picked - lse_pos), 0.0)
        gap = gap * SIM_SCALE
        col = iota((192, 128), 1)
        source = (col // 4) * 6 + core * 3 + col % 4
        picks = ((iota((192, 128), 0) == source) & (col % 4 < 3)).astype(f32)
        gap_own = nn(gap, picks, HIGH)
        for copy in spread:
            copy.wait_send()
        landed[...] = tn(gap_own, questions, HIGH).astype(bf16).reshape(8, 16, WIDTH)
        for copy in gather:
            copy.start()
        sgrad[...] = nn(gap, passages, HIGH)
        r.terms[here] = landed[here]

    def loss_hand():
        for copy in gather:
            copy.wait_recv()
        back[...] = jnp.sum(r.terms[...].astype(f32), axis=0).reshape(4, 4, WIDTH)
        for copy in hand:
            copy.start()

    def loss_back():
        @pl.when(side == 1)
        def _():
            for copy in hand:
                copy.wait_recv()
            summed = jnp.sum(line[...], axis=0)
            for t in range(3):
                sgrad[pl.ds(core * SLOTS + t * 4, 1), :] = summed[t : t + 1]
            send_loss.wait_recv()
            for copy in give:
                copy.wait_send()

        @pl.when(side == 0)
        def _():
            for copy in gather + hand + [swap_p, swap_q, send_loss]:
                copy.wait_send()

        r.losses[...] = r.loss[...]

    n1, roots, low1, f = r.n1, r.roots, r.low1, r.f
    f[...] = nn(ctx[...], wout[...])

    def first_norm(chunk, carry):
        rows = pl.ds(pl.multiple_of(chunk * 256, 256), 256)
        v = f[rows, :] + hid[rows, :].astype(f32) + r.b_out[...]
        v = v - mean_of(v)
        root = lax.rsqrt(mean_of(v * v) + EPS)
        n = v * root
        n1[rows, :] = n.astype(bf16)
        roots[rows, 0:1] = root
        h1 = n * r.ln1_gain[...] + r.ln1_bias[...]
        low1[rows, :] = h1.astype(bf16)
        f[rows, :] = h1 + r.b_down[...]
        return carry

    lax.fori_loop(0, 3, first_norm, 0)

    act, slope = r.act, r.slope
    pl.when(side == 0)(loss_spread)

    def feed(j, carry):
        half, block = j // 3, j % 3
        pl.when((side == 0) & (j == 3))(loss_swap)
        pl.when((side == 0) & (j == 4))(loss_values)
        inner = pl.ds(pl.multiple_of(block * 512, 512), 512)
        cols = pl.ds(pl.multiple_of(j * 512, 512), 512)
        u = nn(low1[...], wup[half, :, inner]) + r.bias_up[half, :, inner]
        for part in range(6):
            rows = pl.ds(part * 128, 128)
            v = u[part * 128 : (part + 1) * 128]
            cdf = 0.5 + 0.5 * lax.erf(v * 0.7071067811865476)
            bell = jnp.exp(v * v * -0.5) * 0.3989422804014327
            act[rows, cols] = (v * cdf).astype(bf16)
            slope[rows, cols] = (cdf + v * bell).astype(bf16)
        a = act[:, cols]
        for part in range(3):
            out = pl.ds(part * 256, 256)
            f[:, out] += nn(a, wdown[half, block, :, :, :, :, out].reshape(512, 256))
        return carry

    lax.fori_loop(0, 6, feed, 0)
    pl.when(side == 0)(loss_hand)

    low2 = r.d_low

    def second_norm(chunk, carry):
        rows = pl.ds(pl.multiple_of(chunk * 256, 256), 256)
        v = f[rows, :]
        v = v - mean_of(v)
        root = lax.rsqrt(mean_of(v * v) + EPS)
        n = v * root
        f[rows, :] = n
        roots[rows, 1:2] = root
        e = (n * r.ln2_gain[...] + r.ln2_bias[...]).astype(bf16)
        low2[rows, :] = e
        return carry

    lax.fori_loop(0, 3, second_norm, 0)
    put_encoded = fetch(low2, r.encoded.at[own_rows])
    mate_encoded = to_mate(low2, r.encoded.at[own_rows])

    loss_back()

    d_low, sums, og = r.d_low, r.sums, r.stage
    put_encoded.wait()
    mate_encoded.wait_send()
    open_sends[:] = [copy for copy in open_sends if copy is not mate_encoded]
    got_grad.wait()
    sums[...] = jnp.zeros_like(sums)

    def second_back(block, carry):
        rows = pl.ds(pl.multiple_of(block * 192, 192), 192)
        whole = og[block // 2, block % 2].reshape(192, WIDTH)
        place = iota((SLOT, WIDTH), 0)
        parts = []
        for part in range(3):
            slot = block * 3 + part
            count_live = r.lengths[core * SLOTS + slot]
            lead = jnp.where((side == 1) & (slot % 4 != 0), 0, 1)
            keep = (place < count_live) & (place >= lead)
            d = jnp.where(keep, whole[part * SLOT : (part + 1) * SLOT].astype(f32), 0.0)
            parts.append(d + jnp.where(place == 0, sgrad[pl.ds(core * SLOTS + slot, 1), :], 0.0))
        d = jnp.concatenate(parts, axis=0)
        n = f[rows, :]
        sums[0] += partial_sum(d * n)
        sums[1] += partial_sum(d)
        d = norm_back(d, n, r.ln2_gain[...], roots[rows, 1:2])
        sums[2] += partial_sum(d)
        f[rows, :] = d
        d_low[rows, :] = d.astype(bf16)
        return carry

    lax.fori_loop(0, 4, second_back, 0)

    where = (x, y, z, device)
    stage = r.stage
    bundles = []

    def start(name, grad, first, finish, apart=False):
        got = [getattr(r, part + name) for part in ("r1_", "r2_", "r3_")]
        b = Bundle(group, where, first, grad, *got, finish, apart)
        bundles.append(b)
        b.advance()
        return b

    def columns(ref, first):
        return ref.at[:, :, :, :, pl.ds(first, HALF)]

    def send_half(name, blocks, make, slot):
        grad = getattr(r, "g_" + name)
        per = 4 // blocks
        moves = []
        for k in range(blocks):
            value = make(1, k).astype(bf16)
            if k > 0:
                moves[k - 1].wait_send()
            slot[...] = value
            moves.append(rc(slot, grad.at[pl.ds(k * per, per)], mate))
            moves[k].start()
        return moves

    def keep_half(name, make, moves):
        grad = getattr(r, "g_" + name)
        per = 4 // len(moves)
        for k, move in enumerate(moves):
            span = pl.ds(k * per, per)
            value = make(0, k)
            move.wait_recv()
            grad[span] = (value + grad[span].astype(f32)).astype(bf16)
        moves[-1].wait_send()

    def make_down(half, k):
        cols = pl.ds(half * 1536 + k * 768, 768)
        return tn(act[:, cols], d_low[...]).reshape(2, 2, 4, 48, WIDTH)

    def end_down(first):
        def finish(part, total):
            r.g_w_down[pl.ds(part * 16, 16), pl.ds(first, HALF)] = total

        return finish

    moves = send_half("down", 2, make_down, stage)

    def feed_back(j, carry):
        half, part = j // 3, j % 3
        inner = pl.ds(pl.multiple_of(part * 512, 512), 512)
        cols = pl.ds(pl.multiple_of(j * 512, 512), 512)
        value = nt(d_low[...], wdown[half, part].reshape(512, WIDTH))
        d = (value * slope[:, cols].astype(f32)).astype(bf16)
        slope[:, cols] = d
        r.sum_up[:, cols] = column_sum(partial_sum(d.astype(f32)))
        for part in range(3):
            out = pl.ds(part * 256, 256)
            f[:, out] += nt(d, wup[half, out, inner])
        return carry

    lax.fori_loop(3, 4, feed_back, 0)
    keep_half("down", make_down, moves)
    down = [
        start("downa", columns(r.g_down, 0), "x", end_down(0), True),
        start("downb", columns(r.g_down, HALF), "y", end_down(HALF), True),
    ]
    lax.fori_loop(4, 6, feed_back, 0)

    def make_up(half, k):
        value = tn(low1[:, pl.ds(k * 384, 384)], slope[:, pl.ds(half * 1536, 1536)])
        left = value[:, :768].reshape(48, 8, WIDTH)
        right = value[:, 768:].reshape(48, 8, WIDTH)
        return jnp.concatenate([left, right], axis=1).reshape(2, 2, 4, 48, WIDTH)

    def end_up(first):
        def finish(part, total):
            rows = pl.ds(part * 8, 8)
            r.g_w_up[rows, pl.ds(first, HALF)] = total[:8]
            r.g_w_up[rows, pl.ds(768 + first, HALF)] = total[8:]

        return finish

    moves = send_half("up", 2, make_up, stage)
    lax.fori_loop(0, 1, feed_back, 0)
    for b in down:
        b.advance()
    lax.fori_loop(1, 3, feed_back, 0)
    pl.semaphore_signal(r.free, inc=1, device_id=mate, device_id_type=MESH)
    keep_half("up", make_up, moves)
    up = [
        start("upa", columns(r.g_up, 0), "x", end_up(0), True),
        start("upb", columns(r.g_up, HALF), "y", end_up(HALF), True),
    ]

    def first_back(chunk, carry):
        rows = pl.ds(pl.multiple_of(chunk * 256, 256), 256)
        d = f[rows, :]
        n = n1[rows, :].astype(f32)
        sums[3] += partial_sum(d * n)
        sums[4] += partial_sum(d)
        d = norm_back(d, n, r.ln1_gain[...], roots[rows, 0:1])
        sums[5] += partial_sum(d)
        f[rows, :] = d
        d_low[rows, :] = d.astype(bf16)
        return carry

    lax.fori_loop(0, 3, first_back, 0)
    for b in down:
        b.advance()

    def make_out(half, k):
        value = tn(ctx[:, pl.ds(half * HALF, HALF)], d_low[...])
        left = value[:, :HALF].reshape(48, 8, HALF)
        right = value[:, HALF:].reshape(48, 8, HALF)
        return jnp.concatenate([left, right], axis=1).reshape(4, 2, 2, 48, HALF)

    def end_out(part, total):
        rows = pl.ds(part * 8, 8)
        r.g_w_out[rows, pl.ds(0, HALF)] = total[:8]
        r.g_w_out[rows, pl.ds(HALF, HALF)] = total[8:]

    moves = send_half("out", 1, make_out, r.stage_out)
    act[:, 0:WIDTH] = nt(d_low[...], wout[...]).astype(bf16)

    def pair_back(pair):
        cols = pl.ds(pl.multiple_of(pair * 128, 128), 128)

        results = []
        for tile in range(3):
            rows = pl.ds(tile * 256, 256)
            q, k, d = qkv[0, rows, cols], qkv[1, rows, cols], act[rows, cols]
            w = weights[pair * 3 + tile]
            dw = nt(split_pair(qkv[2, rows, cols]), d)
            parts = []
            for h in range(2):
                wh = w[h * 256 : (h + 1) * 256].astype(f32)
                dh = dw[h * 256 : (h + 1) * 256]
                parts.append((wh * (dh - column_sum(wh * dh))).astype(bf16))
            ds = jnp.concatenate(parts, axis=0)
            results.append(
                (
                    (tn(ds, split_pair(k)) * 0.125).astype(bf16),
                    merge_pair(nn(ds, q)).astype(bf16),
                    merge_pair(nn(w, d)).astype(bf16),
                )
            )
        for tile in range(3):
            for p in range(3):
                qkv[p, pl.ds(tile * 256, 256), cols] = results[tile][p]
        for k, p in ((6, 0), (7, 2)):
            sums[k, :, cols] = sum(partial_sum(results[tile][p].astype(f32)) for tile in range(3))

    def make_qkv(pair):
        cols = pl.ds(pair * 128, 128)
        d = jnp.concatenate([qkv[p, :, cols] for p in range(3)], axis=1)
        value = tn(hid[...], d).reshape(32, 24, HALF)
        a, b, c = value[:, 0:8], value[:, 8:16], value[:, 16:24]
        top = jnp.concatenate([a, b[:, :, :256]], axis=2)
        low = jnp.concatenate([b[:, :, 256:], c, jnp.zeros((32, 8, 128), f32)], axis=2)
        return jnp.concatenate([top, low], axis=1).reshape(4, 2, 4, 16, 640)

    def end_qkv(pair, first):
        def finish(part, total):
            r.sum_qkv[pair, :, pl.ds(first, total.shape[1])] = total

        return finish

    grad_qkv = [wdown.at[1, k, :, :, :, :, pl.ds(0, 640)] for k in range(3)]
    stage_qkv = [wdown.at[0, k, :, :, :, :, pl.ds(0, 640)] for k in range(3)]
    moves_qkv = [rc(stage_qkv[k], grad_qkv[k], mate) for k in range(3)]
    pl.semaphore_wait(r.free, 1)
    for k in range(3):
        pair_back(3 + k)
        stage_qkv[k][...] = make_qkv(3 + k).astype(bf16)
        moves_qkv[k].start()
        if k == 0:
            keep_half("out", make_out, moves)
            out = start("out", r.g_out, "y", end_out)
        for b in ([], up, down)[k]:
            b.advance()
    last = []
    for k in range(3):
        pair_back(k)
        value = make_qkv(k)
        moves_qkv[k].wait_recv()
        grad_qkv[k][...] = (value + grad_qkv[k][...].astype(f32)).astype(bf16)
        for part, first, start_col, width in (("a", "x", 0, HALF), ("b", "y", HALF, 256)):
            view = wdown.at[1, k, :, :, :, :, pl.ds(start_col, width)]
            last.append(start("qkv%d" % k + part, view, first, end_qkv(k, start_col)))
        for b in ([out], up + down + [out], [])[k]:
            b.advance()
    for k in range(3):
        moves_qkv[k].wait_send()

    vec = r.vec

    def pack(half):
        up = r.sum_up[:, pl.ds(half * 1536, 1536)]
        cols = pl.ds(half * HALF, HALF)
        qv = jnp.concatenate([column_sum(sums[6, :, cols]), column_sum(sums[7, :, cols])], axis=1)
        common = [column_sum(sums[k]) for k in range(6)]
        return jnp.concatenate([up[:, :768], up[:, 768:], qv] + common + [jnp.zeros((7, WIDTH), f32)], axis=0)

    vec[0] = pack(1)
    vec[1] = pack(0)
    vec_mate = to_mate(vec.at[0], vec.at[2])
    vec_state = {}

    def vec_go(buffer, place, ways):
        copies = []
        for way in ways:
            copy = rc(buffer.at[place], buffer.at[place], device(*way))
            copy.start()
            open_sends.append(copy)
            copies.append(copy)
        vec_state["open"] = copies

    def vec_wait():
        for copy in vec_state["open"]:
            copy.wait_recv()

    f[...] += nt(qkv[0], wqkv[0])
    vec_mate.wait_recv()
    r.vec_x[x] = vec[1] + vec[2]
    vec_go(r.vec_x, x, [(0, 0, dx) for dx in (1, 2, 3)])
    for b in last[0:4]:
        b.advance()
    f[...] += nt(qkv[1], wqkv[1])
    for b in [out]:
        b.advance()
    ctx[...] = (f[...] + nt(qkv[2], wqkv[2])).astype(bf16)
    put_grad = fetch(ctx, r.input_grad.at[own_rows])
    mate_grad = to_mate(ctx, r.input_grad.at[own_rows])
    vec_wait()
    r.vec_yz[here] = jnp.sum(r.vec_x[...], axis=0)
    vec_go(r.vec_yz, here, [(dy, dz, 0) for dy, dz in shifts])
    for b in last[4:6] + up + last[0:4]:
        b.advance()
    for b in last[4:6] + up + last[0:4] + last[4:6]:
        b.advance()
    vec_wait()
    r.g_vec[...] = jnp.sum(r.vec_yz[...], axis=0)
    for k in range(3):
        t = r.sum_qkv[k]
        top, low = t[:8], t[8:]
        whole = jnp.concatenate(
            [top[:, :HALF], jnp.concatenate([top[:, HALF:], low[:, :128]], axis=1), low[:, 128:512]], axis=0
        )
        for p in range(3):
            r.g_w_qkv[p, :, pl.ds(k * 128, 128)] = whole[:, p * 128 : (p + 1) * 128]
    put_grad.wait()
    mate_grad.wait_recv()
    mate_encoded.wait_recv()
    for copy in open_sends:
        copy.wait_send()
    assert all(b.done() for b in bundles)
    for b in bundles:
        b.drain()
    assert count.n <= n_copies, count.n


N_COPIES = 91


def layer(lengths, far_in, near_in):
    in_names = ["lengths"] + list(far_in) + list(near_in)
    vmem, far = pl.BlockSpec(memory_space=pltpu.VMEM), pl.BlockSpec(memory_space=pl.ANY)
    in_specs = [pl.BlockSpec(memory_space=pltpu.SMEM)] + [far] * len(far_in) + [vmem] * len(near_in)
    outs = dict(
        encoded=((1536, WIDTH), bf16, far),
        input_grad=((1536, WIDTH), bf16, far),
        losses=((24, 128), f32, vmem),
        g_w_qkv=((3, 24, HALF), f32, vmem),
        g_w_out=((24, WIDTH), f32, vmem),
        g_w_up=((24, 1536), f32, vmem),
        g_w_down=((48, WIDTH), f32, vmem),
        g_vec=((16, WIDTH), f32, vmem),
    )
    scratch = dict(
        hid=((ROWS, WIDTH), bf16),
        wqkv=((3, WIDTH, WIDTH), bf16),
        wout=((WIDTH, WIDTH), bf16),
        wup=((2, WIDTH, 1536), bf16),
        wdown=((2, 3, 4, 2, 4, 16, WIDTH), bf16),
        qkv=((3, ROWS, WIDTH), bf16),
        weights=((18, 512, 256), bf16),
        ctx=((ROWS, WIDTH), bf16),
        n1=((ROWS, WIDTH), bf16),
        low1=((ROWS, WIDTH), bf16),
        act=((ROWS, 3072), bf16),
        slope=((ROWS, 3072), bf16),
        f=((ROWS, WIDTH), f32),
        d_low=((ROWS, WIDTH), bf16),
        roots=((ROWS, 2), f32),
        mask=((ROWS, 256), bf16),
        bias_qv=((2, 2, HALF), f32),
        bias_up=((2, 1, 1536), f32),
        cls=((16, WIDTH), f32),
        mine=((4, WIDTH), f32),
        cls_in=((2, 16, WIDTH), f32),
        cls_low=((16, WIDTH), bf16),
        line=((4, 4, WIDTH), f32),
        back=((4, 4, WIDTH), f32),
        around=((16, WIDTH), bf16),
        landed=((8, 16, WIDTH), bf16),
        terms=((8, 16, WIDTH), bf16),
        sum_qkv=((3, 16, 640), f32),
        g_down=((4, 2, 4, 48, WIDTH), bf16),
        g_up=((4, 2, 4, 48, WIDTH), bf16),
        g_out=((4, 2, 2, 48, HALF), bf16),
        given=((2, 128, WIDTH), bf16),
        ques=((2, 16, WIDTH), bf16),
        loss=((24, 128), f32),
        sgrad=((24, WIDTH), f32),
        sums=((8, 8, WIDTH), f32),
        sum_up=((1, 3072), f32),
        stage=((2, 2, 4, 48, WIDTH), bf16),
        stage_out=((4, 2, 2, 48, HALF), bf16),
        vec=((3, 16, WIDTH), f32),
        vec_x=((4, 16, WIDTH), f32),
        vec_yz=((8, 16, WIDTH), f32),
    )

    def buffers(name, last, rows, cols):
        scratch["r1_" + name] = ((2, last, rows, cols), bf16)
        scratch["r2_" + name] = ((2, 2, last, rows, cols), bf16)
        scratch["r3_" + name] = ((7, rows, cols), bf16)

    for part in "ab":
        buffers("down" + part, 4, 48, HALF)
        buffers("up" + part, 4, 48, HALF)
        for k in range(3):
            buffers("qkv%d" % k + part, 4, 16, HALF if part == "a" else 256)
    buffers("out", 2, 48, HALF)
    sems = dict(
        send=pltpu.SemaphoreType.DMA((N_COPIES,)),
        recv=pltpu.SemaphoreType.DMA((N_COPIES,)),
        lsem=pltpu.SemaphoreType.DMA((10,)),
        free=pltpu.SemaphoreType.REGULAR,
    )
    names = in_names + list(outs) + list(scratch) + list(sems)
    results = pl.pallas_call(
        functools.partial(layer_kernel, N_COPIES, names),
        name="layer",
        out_shape=[jax.ShapeDtypeStruct(shape, kind) for shape, kind, _ in outs.values()],
        in_specs=in_specs,
        out_specs=[spec for _, _, spec in outs.values()],
        scratch_shapes=[pltpu.VMEM(shape, kind) for shape, kind in scratch.values()] + list(sems.values()),
        compiler_params=pltpu.CompilerParams(
            collective_id=0, has_side_effects=True, vmem_limit_bytes=VMEM_LIMIT
        ),
    )(lengths, *far_in.values(), *near_in.values())
    return types.SimpleNamespace(**dict(zip(outs, results)))


VMEM_LIMIT = 64 * 1024 * 1024 - 256 * 1024


def finish_kernel(copies, names, *refs):
    r = types.SimpleNamespace(**dict(zip(names, refs)))
    batch = lax.axis_index("batch")
    moves = []
    for name in copies:
        src, hold, dst = getattr(r, name), getattr(r, "hold_" + name), getattr(r, "out_" + name)
        parts = 4 if src.shape[0] == 1536 else 1
        rows = src.shape[0] // parts
        for part in range(parts):
            span, k = pl.ds(part * rows, rows), len(moves)
            first = pltpu.make_async_copy(src.at[span], hold.at[span], r.sems.at[0, k])
            first.start()
            moves.append((first, pltpu.make_async_copy(hold.at[span], dst.at[span], r.sems.at[1, k])))
    common = pltpu.roll(r.vec[...], (WIDTH - batch * 24) % WIDTH, 1)
    for k, ref in enumerate((r.ln2_gain, r.ln2_bias, r.b_down, r.ln1_gain, r.ln1_bias, r.b_out)):
        ref[...] = common[3 + k : 4 + k, 0:24]
    up = pltpu.roll(r.vec[...], (WIDTH - (batch % 16) * 48) % WIDTH, 1)
    r.b_up[...] = jnp.where(batch < 16, up[0:1, 0:48], up[1:2, 0:48])
    qv = pltpu.roll(r.vec[...], (WIDTH - batch * 12) % WIDTH, 1)
    r.b_qv[0:1, :] = qv[2:3, 0:12]
    r.b_qv[1:2, :] = qv[2:3, HALF : HALF + 12]
    for k in range(12):
        r.out_w_out[k] = r.w_out[pl.ds((batch % 2) * 12 + k, 1), :]
    diagonal = iota((24, 128), 0) == iota((24, 128), 1)
    r.loss[...] = column_sum(jnp.where(diagonal, r.losses[...], 0.0))[:, 0:24]
    for first, second in moves:
        first.wait()
        second.start()
    for _, second in moves:
        second.wait()


def finish(out):
    far, vmem = pl.BlockSpec(memory_space=pl.ANY), pl.BlockSpec(memory_space=pltpu.VMEM)
    large = dict(encoded=out.encoded, input_grad=out.input_grad, w_qkv=out.g_w_qkv, w_up=out.g_w_up, w_down=out.g_w_down)
    small = dict(w_out=out.g_w_out, vec=out.g_vec, losses=out.losses)
    row = jax.ShapeDtypeStruct((1, 24), f32)
    results = dict(
        out_w_out=jax.ShapeDtypeStruct((12, 1, WIDTH), f32),
        b_qv=jax.ShapeDtypeStruct((2, 12), f32),
        b_up=jax.ShapeDtypeStruct((1, 48), f32),
        b_down=row,
        b_out=row,
        ln1_gain=row,
        ln1_bias=row,
        ln2_gain=row,
        ln2_bias=row,
        loss=row,
    )
    moved = {"out_" + name: jax.ShapeDtypeStruct(value.shape, value.dtype) for name, value in large.items()}
    names = list(large) + list(small) + list(moved) + list(results) + ["hold_" + name for name in large] + ["sems"]
    values = pl.pallas_call(
        functools.partial(finish_kernel, list(large), names),
        name="finish",
        out_shape=list(moved.values()) + list(results.values()),
        in_specs=[far] * len(large) + [vmem] * len(small),
        out_specs=[far] * len(moved) + [vmem] * len(results),
        scratch_shapes=[pltpu.VMEM(value.shape, value.dtype) for value in large.values()] + [pltpu.SemaphoreType.DMA((2, 16))],
        compiler_params=pltpu.CompilerParams(vmem_limit_bytes=VMEM_LIMIT),
    )(*large.values(), *small.values())
    return types.SimpleNamespace(**dict(zip(list(moved) + list(results), values)))


def on_device(
    hidden_in, w_qkv, b_qv, w_out, b_out, ln1_gain, ln1_bias, w_up, b_up, w_down, b_down, ln2_gain, ln2_bias, lengths, positives, out_grad
):
    out = layer(
        lengths[0],
        dict(
            hidden_in=hidden_in[0],
            w_qkv=jnp.transpose(w_qkv[0], (1, 0, 2)),
            w_out=w_out[0],
            w_up=w_up[0],
            w_down=w_down[0].reshape(3, 4, 2, 4, 16, WIDTH),
            out_grad=out_grad[0].reshape(2, 2, 2, 4, 48, WIDTH),
        ),
        dict(
            b_qv=b_qv[0],
            b_up=b_up,
            b_out=b_out,
            ln1_gain=ln1_gain,
            ln1_bias=ln1_bias,
            b_down=b_down,
            ln2_gain=ln2_gain,
            ln2_bias=ln2_bias,
            positives=positives,
        ),
    )
    out = finish(out)
    return (
        out.out_encoded[None],
        out.out_input_grad[None],
        out.loss[0],
        jnp.transpose(out.out_w_qkv, (1, 0, 2))[None],
        out.b_qv[None],
        jnp.transpose(out.out_w_out, (1, 0, 2)),
        out.b_out,
        out.ln1_gain,
        out.ln1_bias,
        out.out_w_up[None],
        out.b_up,
        out.out_w_down[None],
        out.b_down,
        out.ln2_gain,
        out.ln2_bias,
    )


def solution(mesh):
    placed = (
        P("side", "batch", None),
        P("side", None, None, "mp"),
        P("side", None, "mp"),
        P("side", "mp", None),
        P("side", None),
        P("side", None),
        P("side", None),
        P("side", None, "mp"),
        P("side", "mp"),
        P("side", "mp", None),
        P("side", None),
        P("side", None),
        P("side", None),
        P("side", "batch"),
        P("batch", None),
        P("side", "batch", None),
    )
    return jax.shard_map(
        on_device,
        mesh=mesh,
        in_specs=placed,
        out_specs=(
            P("side", "batch", None),
            P("side", "batch", None),
            P("batch"),
            P("side", "batch", None, "mp"),
            P("side", None, ("mp", "batch")),
            P("side", ("mp", "batch"), None),
            P("side", "batch"),
            P("side", "batch"),
            P("side", "batch"),
            P("side", "batch", "mp"),
            P("side", ("mp", "batch")),
            P("side", ("mp", "batch"), None),
            P("side", "batch"),
            P("side", "batch"),
            P("side", "batch"),
        ),
        check_vma=False,
    )
```

```python
import functools
import types

import jax
import jax.numpy as jnp
from jax import lax
from jax.experimental import pallas as pl
from jax.experimental.pallas import tpu as pltpu
from jax.sharding import PartitionSpec as P

MESH = pl.DeviceIdType.MESH
bf16 = jnp.bfloat16
f32 = jnp.float32
WIDTH = 768
HALF = 384
ROWS = 768
SLOT = 64
SLOTS = 12
PAIRS = 6
EPS = 1e-05
SIM_SCALE = 0.1
HIGH = lax.Precision.HIGHEST


def nn(a, b, precision=None):
    return lax.dot_general(a, b, (((1,), (0,)), ((), ())), precision=precision, preferred_element_type=f32)


def nt(a, b, precision=None):
    return lax.dot_general(a, b, (((1,), (1,)), ((), ())), precision=precision, preferred_element_type=f32)


def tn(a, b, precision=None):
    return lax.dot_general(a, b, (((0,), (0,)), ((), ())), precision=precision, preferred_element_type=f32)


def iota(shape, axis):
    return lax.broadcasted_iota(jnp.int32, shape, axis)


def split_pair(block):
    first = iota(block.shape, 1) < 64
    zero = jnp.zeros_like(block)
    return jnp.concatenate([jnp.where(first, block, zero), jnp.where(first, zero, block)], axis=0)


def merge_pair(stacked):
    rows = stacked.shape[0] // 2
    first = iota((rows, 128), 1) < 64
    return jnp.where(first, stacked[:rows], stacked[rows:])


def mean_of(values):
    return jnp.sum(values, axis=1, keepdims=True) * (1.0 / WIDTH)


def norm_back(d, n, gain, root):
    u = d * gain
    return (u - mean_of(u) - n * mean_of(u * n)) * root


def partial_sum(values):
    return jnp.sum(values.reshape(values.shape[0] // 8, 8, values.shape[1]), axis=0)


def column_sum(values):
    return jnp.sum(values, axis=0, keepdims=True)


class Counter:
    def __init__(self):
        self.n = 0

    def take(self):
        self.n += 1
        return self.n - 1


class Bundle:
    def __init__(self, group, where, first, grad, r1, r2, r3, finish, apart):
        self.first, self.grad, self.finish, self.apart = first, grad, finish, apart
        self.r1, self.r2, self.r3 = r1, r2, r3
        self.x, self.y, self.z, self.device = where
        self.a = self.y if first == "y" else self.x
        self.b = self.x if first == "y" else self.y
        self.last = grad.shape[2] if first == "y" else grad.shape[0]
        self.step = 0
        far = r3.at[pl.ds(0, self.last)], r3.at[pl.ds(4, 3)]
        self.landing = (r1, r2) + (far if apart else (r3,))
        self.group = [group() for _ in self.landing]

    def index(self, a, z, b):
        return (a, z, b) if self.first == "y" else (b, z, a)

    def piece(self, a, z):
        return self.grad.at[a, z] if self.first == "y" else self.grad.at[:, z, a]

    def to(self, da, dz, db):
        return self.device(da, dz, db) if self.first == "y" else self.device(db, dz, da)

    def owner_b(self, b):
        return b if self.last == 4 else b // 2

    def send(self, step, src, dst, to):
        self.group[step](src, dst, to).start()

    def wait(self, step):
        self.group[step](self.landing[step], self.landing[step], self.to(1, 0, 0)).wait_recv()

    def add(self, where, others):
        def step(k, carry):
            totals = []
            for b in (k * 2, k * 2 + 1):
                total = self.grad[where(b)].astype(f32)
                for ref, index in others(b):
                    total = total + ref[index].astype(f32)
                totals.append(total.astype(bf16))
            for b, total in enumerate(totals):
                self.grad[where(k * 2 + b)] = total
            return carry

        lax.fori_loop(0, self.last // 2, step, 0)

    def advance(self):
        if self.apart:
            (self.step0, self.step1, self.step2z, self.step3z, self.step4)[self.step]()
        else:
            (self.step0, self.step1, self.step2, self.step4)[self.step]()
        self.step += 1

    def done(self):
        return self.step == len(self.landing) + 1

    def step0(self):
        far, up, down = (self.a + 2) % 4, (self.a + 1) % 4, (self.a + 3) % 4
        self.send(0, self.piece(far, 0), self.r1.at[0], self.to(1, 0, 0))
        self.send(0, self.piece(far, 1), self.r1.at[1], self.to(3, 0, 0))
        self.send(1, self.piece(up, 1), self.r2.at[0, 1], self.to(1, 0, 0))
        self.send(1, self.piece(down, 0), self.r2.at[1, 0], self.to(3, 0, 0))

    def step1(self):
        self.wait(0)
        for way, near in ((0, (self.a + 1) % 4), (1, (self.a + 3) % 4)):
            self.add(lambda b: self.index(near, way, b), lambda b: [(self.r1, (way, b))])
            self.send(1, self.piece(near, way), self.r2.at[way, way], self.to((1, 3)[way], 0, 0))

    def own_quarter(self, z):
        self.add(lambda b: self.index(self.a, z, b), lambda b: [(self.r2, (way, z, b)) for way in range(2)])

    def step2(self):
        self.wait(1)
        for z in range(2):
            self.own_quarter(z)
        for dz, db in ((1, 2), (1, 1), (1, 3), (0, 2), (1, 0), (0, 1), (0, 3)):
            src = self.grad.at[self.index(self.a, (self.z + dz) % 2, self.owner_b((self.b + db) % 4))]
            self.send(2, src, self.r3.at[dz * 4 + db - 1], self.to(0, dz, db))

    def step2z(self):
        self.wait(1)
        self.own_quarter(1 - self.z)
        self.send(2, self.piece(self.a, 1 - self.z), self.landing[2], self.to(0, 1, 0))
        self.own_quarter(self.z)

    def step3z(self):
        self.wait(2)
        self.add(lambda b: self.index(self.a, self.z, b), lambda b: [(self.r3, (b,))])
        for db in (2, 1, 3):
            src = self.grad.at[self.index(self.a, self.z, self.owner_b((self.b + db) % 4))]
            self.send(3, src, self.r3.at[3 + db], self.to(0, 0, db))

    def step4(self):
        self.wait(len(self.landing) - 1)
        for part in range(self.grad.shape[3] // 16):
            rows = pl.ds(part * 16, 16)
            total = self.grad[self.index(self.a, self.z, self.owner_b(self.b)) + (rows,)].astype(f32)
            for k in range(4, 7) if self.apart else range(7):
                total = total + self.r3[k, rows].astype(f32)
            self.finish(part, total)

    def drain(self):
        for step, landing in enumerate(self.landing):
            self.group[step](landing, landing, self.to(1, 0, 0)).wait_send()


def layer_kernel(n_copies, near_in, names, *refs):
    r = types.SimpleNamespace(**dict(zip(names, refs)))
    side, batch, core = lax.axis_index("side"), lax.axis_index("batch"), lax.axis_index("mp")
    y, z, x = batch // 8, (batch // 4) % 2, batch % 4

    def device(dy, dz, dx):
        return (side, ((y + dy) % 4) * 8 + ((z + dz) % 2) * 4 + (x + dx) % 4, core)

    def across(dx):
        return (1 - side, y * 8 + z * 4 + (x + dx) % 4, core)

    mate = (side, batch, 1 - core)
    count = Counter()
    local = Counter()
    open_sends = []

    def rc(src, dst, to):
        k = count.take()
        return pltpu.make_async_remote_copy(
            src_ref=src, dst_ref=dst, send_sem=r.send.at[k], recv_sem=r.recv.at[k], device_id=to, device_id_type=MESH
        )

    def group():
        k = count.take()

        def make(src, dst, to):
            return pltpu.make_async_remote_copy(
                src_ref=src, dst_ref=dst, send_sem=r.send.at[k], recv_sem=r.recv.at[k], device_id=to, device_id_type=MESH
            )

        return make

    def to_mate(src, dst):
        copy = rc(src, dst, mate)
        copy.start()
        open_sends.append(copy)
        return copy

    def fetch(src, dst):
        copy = pltpu.make_async_copy(src, dst, r.lsem.at[local.take()])
        copy.start()
        return copy

    hid, wqkv, wout, wup, wdown, qkv = r.hid, r.wqkv, r.wout, r.wup, r.wdown, r.qkv
    own_rows = pl.ds(pl.multiple_of(core * ROWS, ROWS), ROWS)

    barrier = pltpu.get_barrier_semaphore()
    steps = [(dy, dz, 0) for dy in range(4) for dz in range(2)] + [(0, dz, dx) for dz in range(2) for dx in (1, 2, 3)]
    greeted = [mate] + [device(*step) for step in steps[1:]] + [across(dx) for dx in range(4)]
    for to in greeted:
        pl.semaphore_signal(barrier, inc=1, device_id=to, device_id_type=MESH)
    got_lengths = fetch(r.far_lengths, r.lengths)
    got_near = {name: fetch(getattr(r, "far_" + name), getattr(r, name)) for name in near_in}
    got_hid = fetch(r.far_hidden_in.at[own_rows], hid)
    got_qkv = [fetch(r.far_w_qkv.at[p], wqkv.at[p, :, pl.ds(0, HALF)]) for p in range(3)]

    mask = r.mask
    got_lengths.wait()
    for slot in range(SLOTS):
        count_live = r.lengths[core * SLOTS + slot]
        live = iota((SLOT, 256), 0) < count_live
        seen = ((iota((SLOT, 256), 1) // SLOT) == (slot % 4)) | (iota((SLOT, 256), 1) < 256 * side)
        mask[pl.ds(slot * SLOT, SLOT), :] = jnp.where(live & seen, 0.0, -1000000000.0).astype(bf16)

    for copy in got_near.values():
        copy.wait()
    r.bias_qv[0] = r.b_qv[...]
    r.bias_up[0] = r.b_up[...]
    got_hid.wait()

    def project(p, half):
        cols = pl.ds(half * HALF, HALF)
        value = nn(hid[...], wqkv[p, :, cols])
        if p == 0:
            value = (value + r.bias_qv[half, 0:1, :]).astype(bf16) * jnp.asarray(0.125, bf16)
        if p == 2:
            value = value + r.bias_qv[half, 1:2, :]
        qkv[p, :, cols] = value.astype(bf16)

    for p in range(3):
        got_qkv[p].wait()
        project(p, 0)
    pl.semaphore_wait(barrier, len(greeted))
    new_qkv = [to_mate(r.far_w_qkv.at[p], wqkv.at[p, :, pl.ds(HALF, HALF)]) for p in range(3)]
    new_qv = to_mate(r.far_b_qv, r.bias_qv.at[1])
    new_bias = to_mate(r.far_b_up, r.bias_up.at[1])
    got_out = fetch(r.far_w_out, wout.at[pl.ds(0, HALF)])
    got_up = fetch(r.far_w_up, wup.at[0])
    got_down = fetch(r.far_w_down, wdown.at[0])
    got_grad = fetch(r.far_out_grad.at[core], r.stage)

    ctx, weights = r.ctx, r.weights

    def attend(pair, carry):
        cols = pl.ds(pl.multiple_of(pair * 128, 128), 128)
        for tile in range(3):
            rows = pl.ds(tile * 256, 256)
            scores = nt(split_pair(qkv[1, rows, cols]), qkv[0, rows, cols])
            parts = []
            for h in range(2):
                s = scores[h * 256 : (h + 1) * 256] + mask[rows, :].astype(f32)
                e = jnp.exp(s - jnp.max(s, axis=0, keepdims=True))
                parts.append((e * (1.0 / jnp.sum(e, axis=0, keepdims=True))).astype(bf16))
            w = jnp.concatenate(parts, axis=0)
            weights[pair * 3 + tile] = w
            ctx[rows, cols] = tn(w, split_pair(qkv[2, rows, cols])).astype(bf16)
        return carry

    lax.fori_loop(0, 2, attend, 0)
    for copy in new_qkv:
        copy.wait_send()
    open_sends[:] = [copy for copy in open_sends if not any(copy is other for other in new_qkv)]
    new_out = to_mate(r.far_w_out, wout.at[pl.ds(HALF, HALF)])
    new_up = to_mate(r.far_w_up, wup.at[1])
    new_down = to_mate(r.far_w_down, wdown.at[1])
    lax.fori_loop(2, 3, attend, 0)
    new_qv.wait_recv()
    for p in range(3):
        new_qkv[p].wait_recv()
        project(p, 1)
    lax.fori_loop(3, PAIRS, attend, 0)

    cls, line, landed, back, sgrad = r.cls, r.line, r.landed, r.back, r.sgrad
    r.cls_in[...] = jnp.zeros_like(r.cls_in)
    for slot in range(SLOTS):
        rows = pl.ds(slot * SLOT, 16)
        r.cls_in[0, slot : slot + 1, :] = ctx[rows, :].astype(f32)[0:1]
        r.cls_in[1, slot : slot + 1, :] = hid[rows, :].astype(f32)[0:1]
    got_out.wait()
    new_out.wait_recv()
    v = nn(r.cls_in[0].astype(bf16), wout[...]) + r.cls_in[1] + r.b_out[...]
    v = v - mean_of(v)
    v = v * lax.rsqrt(mean_of(v * v) + EPS) * r.ln1_gain[...] + r.ln1_bias[...]
    r.cls_low[...] = v.astype(bf16)
    cls[...] = v + r.b_down[...]
    got_up.wait()
    got_down.wait()
    new_up.wait_recv()
    new_down.wait_recv()
    new_bias.wait_recv()

    def feed_cls(j, carry):
        half, part = j // 3, j % 3
        inner = pl.ds(pl.multiple_of(part * 512, 512), 512)
        u = nn(r.cls_low[...], wup[half, :, inner]) + r.bias_up[half, :, inner]
        a = (u * (0.5 + 0.5 * lax.erf(u * 0.7071067811865476))).astype(bf16)
        cls[...] += nn(a, wdown[half, part].reshape(512, WIDTH))
        return carry

    lax.fori_loop(0, 6, feed_cls, 0)
    v = cls[...]
    v = v - mean_of(v)
    v = v * lax.rsqrt(mean_of(v * v) + EPS) * r.ln2_gain[...] + r.ln2_bias[...]
    cls[...] = v.astype(bf16).astype(f32)

    shifts = [(dy, dz) for dy in range(4) for dz in range(2)][1:]
    here = y * 2 + z
    give = [rc(r.mine, line.at[x], across(dx)) for dx in range(4)]
    spread = [rc(r.around, landed.at[here], device(dy, dz, 0)) for dy, dz in shifts]
    gather = [rc(landed.at[((y + dy) % 4) * 2 + ((z + dz) % 2)], r.terms.at[here], device(dy, dz, 0)) for dy, dz in shifts]
    hand = [rc(back.at[(x + dx) % 4], line.at[x], across(dx)) for dx in range(4)]
    swap_p = rc(r.given.at[0], r.given.at[1], mate)
    swap_q = rc(r.ques.at[0], r.ques.at[1], mate)
    send_loss = rc(r.loss, r.loss, across(0))
    sgrad[...] = jnp.zeros_like(sgrad)

    @pl.when(side == 1)
    def _():
        for t in range(3):
            r.mine[pl.ds(t, 1), :] = cls[pl.ds(t * 4, 1), :]
        r.mine[pl.ds(3, 1), :] = cls[pl.ds(0, 1), :]
        for copy in give:
            copy.start()

    @pl.when(side == 0)
    def _():
        r.ques[0] = cls[...].astype(bf16)
        swap_q.start()

    def loss_spread():
        for copy in give:
            copy.wait_recv()
        r.around[...] = line[...].reshape(16, WIDTH).astype(bf16)
        for copy in spread:
            copy.start()
        landed[here] = r.around[...]

    def loss_swap():
        for copy in spread:
            copy.wait_recv()
        r.given[0] = landed[...].reshape(128, WIDTH)
        swap_p.start()

    def loss_values():
        swap_q.wait_recv()
        place = iota((32, 32), 0)
        home = (place // SLOTS) ^ core
        wanted = home * 16 + place % SLOTS
        picks = ((iota((32, 32), 1) == wanted) & (place < 24)).astype(bf16)
        questions = nn(picks, r.ques[...].reshape(32, WIDTH))[0:24]
        swap_p.wait_recv()
        col = iota((192, 256), 0)
        chip, inner = col // 6, col % 6
        owner = inner // 3
        spot = (owner ^ core) * 128 + chip * 4 + inner % 3
        picks = (iota((192, 256), 1) == spot).astype(bf16)
        passages = nn(picks, r.given[...].reshape(256, WIDTH))
        sims = nt(questions.astype(bf16), passages.astype(bf16)) * SIM_SCALE
        chosen = r.positives[...] > 0
        top = jnp.max(sims, axis=1, keepdims=True)
        lse_all = top + jnp.log(jnp.sum(jnp.exp(sims - top), axis=1, keepdims=True))
        picked = jnp.where(chosen, sims, -1000000000.0)
        top_pos = jnp.max(picked, axis=1, keepdims=True)
        lse_pos = top_pos + jnp.log(jnp.sum(jnp.exp(picked - top_pos), axis=1, keepdims=True))
        r.loss[...] = jnp.broadcast_to(lse_all - lse_pos, (24, 128))
        send_loss.start()
        gap = jnp.exp(sims - lse_all) - jnp.where(chosen, jnp.exp(picked - lse_pos), 0.0)
        gap = gap * SIM_SCALE
        col = iota((192, 128), 1)
        source = (col // 4) * 6 + core * 3 + col % 4
        picks = ((iota((192, 128), 0) == source) & (col % 4 < 3)).astype(f32)
        gap_own = nn(gap, picks, HIGH)
        for copy in spread:
            copy.wait_send()
        landed[...] = tn(gap_own, questions, HIGH).astype(bf16).reshape(8, 16, WIDTH)
        for copy in gather:
            copy.start()
        sgrad[...] = nn(gap, passages, HIGH)
        r.terms[here] = landed[here]

    def loss_hand():
        for copy in gather:
            copy.wait_recv()
        back[...] = jnp.sum(r.terms[...].astype(f32), axis=0).reshape(4, 4, WIDTH)
        for copy in hand:
            copy.start()

    def loss_back():
        @pl.when(side == 1)
        def _():
            for copy in hand:
                copy.wait_recv()
            summed = jnp.sum(line[...], axis=0)
            for t in range(3):
                sgrad[pl.ds(core * SLOTS + t * 4, 1), :] = summed[t : t + 1]
            send_loss.wait_recv()
            for copy in give:
                copy.wait_send()

        @pl.when(side == 0)
        def _():
            for copy in gather + hand + [swap_p, swap_q, send_loss]:
                copy.wait_send()


    n1, roots, low1, f = r.n1, r.roots, r.low1, r.f
    f[...] = nn(ctx[...], wout[...])

    def first_norm(chunk, carry):
        rows = pl.ds(pl.multiple_of(chunk * 256, 256), 256)
        v = f[rows, :] + hid[rows, :].astype(f32) + r.b_out[...]
        v = v - mean_of(v)
        root = lax.rsqrt(mean_of(v * v) + EPS)
        n = v * root
        n1[rows, :] = n.astype(bf16)
        roots[rows, 0:1] = root
        h1 = n * r.ln1_gain[...] + r.ln1_bias[...]
        low1[rows, :] = h1.astype(bf16)
        f[rows, :] = h1 + r.b_down[...]
        return carry

    lax.fori_loop(0, 3, first_norm, 0)

    act, slope = r.act, r.slope

    def feed(j, carry):
        half, block = j // 3, j % 3
        pl.when((side == 0) & (j == 1))(loss_spread)
        pl.when((side == 0) & (j == 4))(loss_swap)
        pl.when((side == 0) & (j == 5))(loss_values)
        inner = pl.ds(pl.multiple_of(block * 512, 512), 512)
        cols = pl.ds(pl.multiple_of(j * 512, 512), 512)
        u = nn(low1[...], wup[half, :, inner]) + r.bias_up[half, :, inner]
        for part in range(6):
            rows = pl.ds(part * 128, 128)
            v = u[part * 128 : (part + 1) * 128]
            cdf = 0.5 + 0.5 * lax.erf(v * 0.7071067811865476)
            bell = jnp.exp(v * v * -0.5) * 0.3989422804014327
            act[rows, cols] = (v * cdf).astype(bf16)
            slope[rows, cols] = (cdf + v * bell).astype(bf16)
        a = act[:, cols]
        for part in range(3):
            out = pl.ds(part * 256, 256)
            f[:, out] += nn(a, wdown[half, block, :, :, :, :, out].reshape(512, 256))
        return carry

    lax.fori_loop(0, 6, feed, 0)

    low2 = r.d_low

    def second_norm(chunk, carry):
        rows = pl.ds(pl.multiple_of(chunk * 256, 256), 256)
        v = f[rows, :]
        v = v - mean_of(v)
        root = lax.rsqrt(mean_of(v * v) + EPS)
        n = v * root
        f[rows, :] = n
        roots[rows, 1:2] = root
        e = (n * r.ln2_gain[...] + r.ln2_bias[...]).astype(bf16)
        low2[rows, :] = e
        return carry

    lax.fori_loop(0, 3, second_norm, 0)
    put_encoded = fetch(low2, r.far_encoded.at[own_rows])
    mate_encoded = to_mate(low2, r.far_encoded.at[own_rows])

    pl.when(side == 0)(loss_hand)
    loss_back()
    puts = [fetch(r.loss, r.far_loss)]

    d_low, sums, og = r.d_low, r.sums, r.stage
    put_encoded.wait()
    mate_encoded.wait_send()
    open_sends[:] = [copy for copy in open_sends if copy is not mate_encoded]
    got_grad.wait()
    sums[...] = jnp.zeros_like(sums)

    def second_back(block, carry):
        rows = pl.ds(pl.multiple_of(block * 192, 192), 192)
        whole = og[block // 2, block % 2].reshape(192, WIDTH)
        place = iota((SLOT, WIDTH), 0)
        parts = []
        for part in range(3):
            slot = block * 3 + part
            count_live = r.lengths[core * SLOTS + slot]
            lead = jnp.where((side == 1) & (slot % 4 != 0), 0, 1)
            keep = (place < count_live) & (place >= lead)
            d = jnp.where(keep, whole[part * SLOT : (part + 1) * SLOT].astype(f32), 0.0)
            parts.append(d + jnp.where(place == 0, sgrad[pl.ds(core * SLOTS + slot, 1), :], 0.0))
        d = jnp.concatenate(parts, axis=0)
        n = f[rows, :]
        sums[0] += partial_sum(d * n)
        sums[1] += partial_sum(d)
        d = norm_back(d, n, r.ln2_gain[...], roots[rows, 1:2])
        sums[2] += partial_sum(d)
        f[rows, :] = d
        d_low[rows, :] = d.astype(bf16)
        return carry

    lax.fori_loop(0, 4, second_back, 0)

    where = (x, y, z, device)
    stage = r.stage
    bundles = []

    def start(name, grad, first, finish, apart=False):
        got = [getattr(r, part + name) for part in ("r1_", "r2_", "r3_")]
        b = Bundle(group, where, first, grad, *got, finish, apart)
        bundles.append(b)
        b.advance()
        return b

    def columns(ref, first):
        return ref.at[:, :, :, :, pl.ds(first, HALF)]

    def send_half(name, blocks, make, slot):
        grad = getattr(r, "g_" + name)
        per = 4 // blocks
        moves = []
        for k in range(blocks):
            value = make(1, k).astype(bf16)
            if k > 0:
                moves[k - 1].wait_send()
            slot[...] = value
            moves.append(rc(slot, grad.at[pl.ds(k * per, per)], mate))
            moves[k].start()
        return moves

    def keep_half(name, make, moves):
        grad = getattr(r, "g_" + name)
        per = 4 // len(moves)
        for k, move in enumerate(moves):
            span = pl.ds(k * per, per)
            value = make(0, k)
            move.wait_recv()
            grad[span] = (value + grad[span].astype(f32)).astype(bf16)
        moves[-1].wait_send()

    def make_down(half, k):
        cols = pl.ds(half * 1536 + k * 768, 768)
        return tn(act[:, cols], d_low[...]).reshape(2, 2, 4, 48, WIDTH)

    def end_down(first):
        def finish(part, total):
            r.g_w_down[pl.ds(part * 16, 16), pl.ds(first, HALF)] = total

        return finish

    moves = send_half("down", 2, make_down, stage)

    def feed_back(j, carry):
        half, part = j // 3, j % 3
        inner = pl.ds(pl.multiple_of(part * 512, 512), 512)
        cols = pl.ds(pl.multiple_of(j * 512, 512), 512)
        value = nt(d_low[...], wdown[half, part].reshape(512, WIDTH))
        d = (value * slope[:, cols].astype(f32)).astype(bf16)
        slope[:, cols] = d
        r.sum_up[:, cols] = column_sum(partial_sum(d.astype(f32)))
        for part in range(3):
            out = pl.ds(part * 256, 256)
            f[:, out] += nt(d, wup[half, out, inner])
        return carry

    lax.fori_loop(3, 4, feed_back, 0)
    keep_half("down", make_down, moves)
    down = [
        start("downa", columns(r.g_down, 0), "x", end_down(0), True),
        start("downb", columns(r.g_down, HALF), "y", end_down(HALF), True),
    ]
    lax.fori_loop(4, 6, feed_back, 0)

    def make_up(half, k):
        value = tn(low1[:, pl.ds(k * 384, 384)], slope[:, pl.ds(half * 1536, 1536)])
        left = value[:, :768].reshape(48, 8, WIDTH)
        right = value[:, 768:].reshape(48, 8, WIDTH)
        return jnp.concatenate([left, right], axis=1).reshape(2, 2, 4, 48, WIDTH)

    def end_up(first):
        def finish(part, total):
            rows = pl.ds(part * 8, 8)
            r.g_w_up[rows, pl.ds(first, HALF)] = total[:8]
            r.g_w_up[rows, pl.ds(768 + first, HALF)] = total[8:]

        return finish

    moves = send_half("up", 2, make_up, stage)
    lax.fori_loop(0, 1, feed_back, 0)
    for b in down:
        b.advance()
    lax.fori_loop(1, 3, feed_back, 0)
    pl.semaphore_signal(r.free, inc=1, device_id=mate, device_id_type=MESH)
    keep_half("up", make_up, moves)
    up = [
        start("upa", columns(r.g_up, 0), "x", end_up(0), True),
        start("upb", columns(r.g_up, HALF), "y", end_up(HALF), True),
    ]

    def first_back(chunk, carry):
        rows = pl.ds(pl.multiple_of(chunk * 256, 256), 256)
        d = f[rows, :]
        n = n1[rows, :].astype(f32)
        sums[3] += partial_sum(d * n)
        sums[4] += partial_sum(d)
        d = norm_back(d, n, r.ln1_gain[...], roots[rows, 0:1])
        sums[5] += partial_sum(d)
        f[rows, :] = d
        d_low[rows, :] = d.astype(bf16)
        return carry

    lax.fori_loop(0, 3, first_back, 0)
    for b in down:
        b.advance()

    def make_out(half, k):
        value = tn(ctx[:, pl.ds(half * HALF, HALF)], d_low[...])
        left = value[:, :HALF].reshape(48, 8, HALF)
        right = value[:, HALF:].reshape(48, 8, HALF)
        return jnp.concatenate([left, right], axis=1).reshape(4, 2, 2, 48, HALF)

    def end_out(part, total):
        rows = pl.ds(part * 8, 8)
        r.g_w_out[rows, pl.ds(0, HALF)] = total[:8]
        r.g_w_out[rows, pl.ds(HALF, HALF)] = total[8:]

    moves = send_half("out", 1, make_out, r.stage_out)
    act[:, 0:WIDTH] = nt(d_low[...], wout[...]).astype(bf16)

    def pair_back(pair):
        cols = pl.ds(pl.multiple_of(pair * 128, 128), 128)

        results = []
        for tile in range(3):
            rows = pl.ds(tile * 256, 256)
            q, k, d = qkv[0, rows, cols], qkv[1, rows, cols], act[rows, cols]
            w = weights[pair * 3 + tile]
            dw = nt(split_pair(qkv[2, rows, cols]), d)
            parts = []
            for h in range(2):
                wh = w[h * 256 : (h + 1) * 256].astype(f32)
                dh = dw[h * 256 : (h + 1) * 256]
                parts.append((wh * (dh - column_sum(wh * dh))).astype(bf16))
            ds = jnp.concatenate(parts, axis=0)
            results.append(
                (
                    (tn(ds, split_pair(k)) * 0.125).astype(bf16),
                    merge_pair(nn(ds, q)).astype(bf16),
                    merge_pair(nn(w, d)).astype(bf16),
                )
            )
        for tile in range(3):
            for p in range(3):
                qkv[p, pl.ds(tile * 256, 256), cols] = results[tile][p]
        for k, p in ((6, 0), (7, 2)):
            sums[k, :, cols] = sum(partial_sum(results[tile][p].astype(f32)) for tile in range(3))

    def make_qkv(pair):
        cols = pl.ds(pair * 128, 128)
        d = jnp.concatenate([qkv[p, :, cols] for p in range(3)], axis=1)
        value = tn(hid[...], d).reshape(32, 24, HALF)
        a, b, c = value[:, 0:8], value[:, 8:16], value[:, 16:24]
        top = jnp.concatenate([a, b[:, :, :256]], axis=2)
        low = jnp.concatenate([b[:, :, 256:], c, jnp.zeros((32, 8, 128), f32)], axis=2)
        return jnp.concatenate([top, low], axis=1).reshape(4, 2, 4, 16, 640)

    def end_qkv(pair, first):
        def finish(part, total):
            r.sum_qkv[pair, :, pl.ds(first, total.shape[1])] = total

        return finish

    grad_qkv = [wdown.at[1, k, :, :, :, :, pl.ds(0, 640)] for k in range(3)]
    stage_qkv = [wdown.at[0, k, :, :, :, :, pl.ds(0, 640)] for k in range(3)]
    moves_qkv = [rc(stage_qkv[k], grad_qkv[k], mate) for k in range(3)]
    pl.semaphore_wait(r.free, 1)
    for k in range(3):
        pair_back(3 + k)
        stage_qkv[k][...] = make_qkv(3 + k).astype(bf16)
        moves_qkv[k].start()
        if k == 0:
            keep_half("out", make_out, moves)
            out = start("out", r.g_out, "y", end_out)
    last = []
    for k in range(3):
        pair_back(k)
        value = make_qkv(k)
        moves_qkv[k].wait_recv()
        grad_qkv[k][...] = (value + grad_qkv[k][...].astype(f32)).astype(bf16)
        for part, first, start_col, width in (("a", "x", 0, HALF), ("b", "y", HALF, 256)):
            view = wdown.at[1, k, :, :, :, :, pl.ds(start_col, width)]
            last.append(start("qkv%d" % k + part, view, first, end_qkv(k, start_col)))
        for b in (up + down, [out], up)[k]:
            b.advance()
    for k in range(3):
        moves_qkv[k].wait_send()

    vec = r.vec

    def pack(half):
        up = r.sum_up[:, pl.ds(half * 1536, 1536)]
        cols = pl.ds(half * HALF, HALF)
        qv = jnp.concatenate([column_sum(sums[6, :, cols]), column_sum(sums[7, :, cols])], axis=1)
        common = [column_sum(sums[k]) for k in range(6)]
        return jnp.concatenate([up[:, :768], up[:, 768:], qv] + common + [jnp.zeros((7, WIDTH), f32)], axis=0)

    vec[0] = pack(1)
    vec[1] = pack(0)
    vec_mate = to_mate(vec.at[0], vec.at[2])
    vec_state = {}

    def vec_go(buffer, place, ways):
        copies = []
        for way in ways:
            copy = rc(buffer.at[place], buffer.at[place], device(*way))
            copy.start()
            open_sends.append(copy)
            copies.append(copy)
        vec_state["open"] = copies

    def vec_wait():
        for copy in vec_state["open"]:
            copy.wait_recv()

    f[...] += nt(qkv[0], wqkv[0])
    vec_mate.wait_recv()
    r.vec_x[x] = vec[1] + vec[2]
    vec_go(r.vec_x, x, [(0, 0, dx) for dx in (1, 2, 3)])
    for b in last[0:4]:
        b.advance()
    f[...] += nt(qkv[1], wqkv[1])
    for b in [out] + down:
        b.advance()
    ctx[...] = (f[...] + nt(qkv[2], wqkv[2])).astype(bf16)
    put_grad = fetch(ctx, r.far_input_grad.at[own_rows])
    mate_grad = to_mate(ctx, r.far_input_grad.at[own_rows])
    for b in last[4:6]:
        b.advance()
    vec_wait()
    r.vec_yz[here] = jnp.sum(r.vec_x[...], axis=0)
    vec_go(r.vec_yz, here, [(dy, dz, 0) for dy, dz in shifts])
    for b in last[0:4] + up + last[4:6] + [out] + last[0:4] + up + last[4:6]:
        b.advance()
    vec_wait()
    r.g_vec[...] = jnp.sum(r.vec_yz[...], axis=0)
    for k in range(3):
        t = r.sum_qkv[k]
        top, low = t[:8], t[8:]
        whole = jnp.concatenate(
            [top[:, :HALF], jnp.concatenate([top[:, HALF:], low[:, :128]], axis=1), low[:, 128:512]], axis=0
        )
        for p in range(3):
            r.g_w_qkv[p, :, pl.ds(k * 128, 128)] = whole[:, p * 128 : (p + 1) * 128]
    puts += [fetch(getattr(r, name), getattr(r, "far_" + name)) for name in ("g_w_qkv", "g_w_out", "g_w_up", "g_w_down", "g_vec")]
    put_grad.wait()
    for copy in puts:
        copy.wait()
    mate_grad.wait_recv()
    mate_encoded.wait_recv()
    for copy in open_sends:
        copy.wait_send()
    assert all(b.done() for b in bundles)
    for b in bundles:
        b.drain()
    assert count.n <= n_copies and local.n <= 26


N_COPIES = 91


def layer(lengths, far_in, near_in):
    far = pl.BlockSpec(memory_space=pl.ANY)
    outs = dict(
        encoded=((1536, WIDTH), bf16),
        input_grad=((1536, WIDTH), bf16),
        loss=((24, 128), f32),
        g_w_qkv=((3, 24, HALF), f32),
        g_w_out=((24, WIDTH), f32),
        g_w_up=((24, 1536), f32),
        g_w_down=((48, WIDTH), f32),
        g_vec=((16, WIDTH), f32),
    )
    scratch = dict(
        hid=((ROWS, WIDTH), bf16),
        wqkv=((3, WIDTH, WIDTH), bf16),
        wout=((WIDTH, WIDTH), bf16),
        wup=((2, WIDTH, 1536), bf16),
        wdown=((2, 3, 4, 2, 4, 16, WIDTH), bf16),
        qkv=((3, ROWS, WIDTH), bf16),
        weights=((18, 512, 256), bf16),
        ctx=((ROWS, WIDTH), bf16),
        n1=((ROWS, WIDTH), bf16),
        low1=((ROWS, WIDTH), bf16),
        act=((ROWS, 3072), bf16),
        slope=((ROWS, 3072), bf16),
        f=((ROWS, WIDTH), f32),
        d_low=((ROWS, WIDTH), bf16),
        roots=((ROWS, 2), f32),
        mask=((ROWS, 256), bf16),
        bias_qv=((2, 2, HALF), f32),
        bias_up=((2, 1, 1536), f32),
        cls=((16, WIDTH), f32),
        mine=((4, WIDTH), f32),
        cls_in=((2, 16, WIDTH), f32),
        cls_low=((16, WIDTH), bf16),
        line=((4, 4, WIDTH), f32),
        back=((4, 4, WIDTH), f32),
        around=((16, WIDTH), bf16),
        landed=((8, 16, WIDTH), bf16),
        terms=((8, 16, WIDTH), bf16),
        sum_qkv=((3, 16, 640), f32),
        g_down=((4, 2, 4, 48, WIDTH), bf16),
        g_up=((4, 2, 4, 48, WIDTH), bf16),
        g_out=((4, 2, 2, 48, HALF), bf16),
        given=((2, 128, WIDTH), bf16),
        ques=((2, 16, WIDTH), bf16),
        sgrad=((24, WIDTH), f32),
        sums=((8, 8, WIDTH), f32),
        sum_up=((1, 3072), f32),
        stage=((2, 2, 4, 48, WIDTH), bf16),
        stage_out=((4, 2, 2, 48, HALF), bf16),
        vec=((3, 16, WIDTH), f32),
        vec_x=((4, 16, WIDTH), f32),
        vec_yz=((8, 16, WIDTH), f32),
    )

    def buffers(name, last, rows, cols):
        scratch["r1_" + name] = ((2, last, rows, cols), bf16)
        scratch["r2_" + name] = ((2, 2, last, rows, cols), bf16)
        scratch["r3_" + name] = ((7, rows, cols), bf16)

    for part in "ab":
        buffers("down" + part, 4, 48, HALF)
        buffers("up" + part, 4, 48, HALF)
        for k in range(3):
            buffers("qkv%d" % k + part, 4, 16, HALF if part == "a" else 256)
    buffers("out", 2, 48, HALF)
    sems = dict(
        send=pltpu.SemaphoreType.DMA((N_COPIES,)),
        recv=pltpu.SemaphoreType.DMA((N_COPIES,)),
        lsem=pltpu.SemaphoreType.DMA((26,)),
        free=pltpu.SemaphoreType.REGULAR,
    )
    for name, value in near_in.items():
        scratch[name] = (value.shape, value.dtype)
    for name, (shape, kind) in outs.items():
        if kind == f32:
            scratch[name] = (shape, kind)
    sems["lengths"] = pltpu.SMEM(lengths.shape, jnp.int32)
    names = ["far_" + name for name in ["lengths"] + list(far_in) + list(near_in) + list(outs)] + list(scratch) + list(sems)
    results = pl.pallas_call(
        functools.partial(layer_kernel, N_COPIES, list(near_in), names),
        name="layer",
        out_shape=[jax.ShapeDtypeStruct(shape, kind) for shape, kind in outs.values()],
        in_specs=[far] * (1 + len(far_in) + len(near_in)),
        out_specs=[far] * len(outs),
        scratch_shapes=[pltpu.VMEM(shape, kind) for shape, kind in scratch.values()] + list(sems.values()),
        compiler_params=pltpu.CompilerParams(
            collective_id=0, has_side_effects=True, vmem_limit_bytes=VMEM_LIMIT
        ),
    )(lengths, *far_in.values(), *near_in.values())
    return types.SimpleNamespace(**dict(zip(outs, results)))


VMEM_LIMIT = 64 * 1024 * 1024 - 256 * 1024


def finish_kernel(copies, names, *refs):
    r = types.SimpleNamespace(**dict(zip(names, refs)))
    batch = lax.axis_index("batch")
    near = []
    for name in ("vec", "w_out", "losses"):
        copy = pltpu.make_async_copy(getattr(r, name), getattr(r, "near_" + name), r.sems.at[0, 12 + len(near)])
        copy.start()
        near.append(copy)
    moves = []
    for name in copies:
        src, hold, dst = getattr(r, name), getattr(r, "hold_" + name), getattr(r, "out_" + name)
        parts = 4 if src.shape[0] == 1536 else 1
        rows = src.shape[0] // parts
        for part in range(parts):
            span, k = pl.ds(part * rows, rows), len(moves)
            first = pltpu.make_async_copy(src.at[span], hold.at[span], r.sems.at[0, k])
            first.start()
            moves.append((first, pltpu.make_async_copy(hold.at[span], dst.at[span], r.sems.at[1, k])))
    for first, second in moves:
        first.wait()
        second.start()
    for copy in near:
        copy.wait()
    common = pltpu.roll(r.near_vec[...], (WIDTH - batch * 24) % WIDTH, 1)
    for k, ref in enumerate((r.ln2_gain, r.ln2_bias, r.b_down, r.ln1_gain, r.ln1_bias, r.b_out)):
        ref[...] = common[3 + k : 4 + k, 0:24]
    up = pltpu.roll(r.near_vec[...], (WIDTH - (batch % 16) * 48) % WIDTH, 1)
    r.b_up[...] = jnp.where(batch < 16, up[0:1, 0:48], up[1:2, 0:48])
    qv = pltpu.roll(r.near_vec[...], (WIDTH - batch * 12) % WIDTH, 1)
    r.b_qv[0:1, :] = qv[2:3, 0:12]
    r.b_qv[1:2, :] = qv[2:3, HALF : HALF + 12]
    for k in range(12):
        r.out_w_out[k] = r.near_w_out[pl.ds((batch % 2) * 12 + k, 1), :]
    diagonal = iota((24, 128), 0) == iota((24, 128), 1)
    r.loss[...] = column_sum(jnp.where(diagonal, r.near_losses[...], 0.0))[:, 0:24]
    for _, second in moves:
        second.wait()


def finish(out):
    far, vmem = pl.BlockSpec(memory_space=pl.ANY), pl.BlockSpec(memory_space=pltpu.VMEM)
    large = dict(encoded=out.encoded, input_grad=out.input_grad, w_qkv=out.g_w_qkv, w_up=out.g_w_up, w_down=out.g_w_down)
    small = dict(vec=out.g_vec, w_out=out.g_w_out, losses=out.loss)
    row = jax.ShapeDtypeStruct((1, 24), f32)
    results = dict(
        out_w_out=jax.ShapeDtypeStruct((12, 1, WIDTH), f32),
        b_qv=jax.ShapeDtypeStruct((2, 12), f32),
        b_up=jax.ShapeDtypeStruct((1, 48), f32),
        b_down=row,
        b_out=row,
        ln1_gain=row,
        ln1_bias=row,
        ln2_gain=row,
        ln2_bias=row,
        loss=row,
    )
    moved = {"out_" + name: jax.ShapeDtypeStruct(value.shape, value.dtype) for name, value in large.items()}
    names = list(large) + list(small) + list(moved) + list(results) + ["hold_" + name for name in large] + ["near_" + name for name in small] + ["sems"]
    values = pl.pallas_call(
        functools.partial(finish_kernel, list(large), names),
        name="finish",
        out_shape=list(moved.values()) + list(results.values()),
        in_specs=[far] * (len(large) + len(small)),
        out_specs=[far] * len(moved) + [vmem] * len(results),
        scratch_shapes=[pltpu.VMEM(value.shape, value.dtype) for value in (large | small).values()] + [pltpu.SemaphoreType.DMA((2, 16))],
        compiler_params=pltpu.CompilerParams(vmem_limit_bytes=VMEM_LIMIT),
    )(*large.values(), *small.values())
    return types.SimpleNamespace(**dict(zip(list(moved) + list(results), values)))


def on_device(
    hidden_in, w_qkv, b_qv, w_out, b_out, ln1_gain, ln1_bias, w_up, b_up, w_down, b_down, ln2_gain, ln2_bias, lengths, positives, out_grad
):
    out = layer(
        lengths[0],
        dict(
            hidden_in=hidden_in[0],
            w_qkv=jnp.transpose(w_qkv[0], (1, 0, 2)),
            w_out=w_out[0],
            w_up=w_up[0],
            w_down=w_down[0].reshape(3, 4, 2, 4, 16, WIDTH),
            out_grad=out_grad[0].reshape(2, 2, 2, 4, 48, WIDTH),
        ),
        dict(
            b_qv=b_qv[0],
            b_up=b_up,
            b_out=b_out,
            ln1_gain=ln1_gain,
            ln1_bias=ln1_bias,
            b_down=b_down,
            ln2_gain=ln2_gain,
            ln2_bias=ln2_bias,
            positives=positives,
        ),
    )
    out = finish(out)
    return (
        out.out_encoded[None],
        out.out_input_grad[None],
        out.loss[0],
        jnp.transpose(out.out_w_qkv, (1, 0, 2))[None],
        out.b_qv[None],
        jnp.transpose(out.out_w_out, (1, 0, 2)),
        out.b_out,
        out.ln1_gain,
        out.ln1_bias,
        out.out_w_up[None],
        out.b_up,
        out.out_w_down[None],
        out.b_down,
        out.ln2_gain,
        out.ln2_bias,
    )


def solution(mesh):
    placed = (
        P("side", "batch", None),
        P("side", None, None, "mp"),
        P("side", None, "mp"),
        P("side", "mp", None),
        P("side", None),
        P("side", None),
        P("side", None),
        P("side", None, "mp"),
        P("side", "mp"),
        P("side", "mp", None),
        P("side", None),
        P("side", None),
        P("side", None),
        P("side", "batch"),
        P("batch", None),
        P("side", "batch", None),
    )
    return jax.shard_map(
        on_device,
        mesh=mesh,
        in_specs=placed,
        out_specs=(
            P("side", "batch", None),
            P("side", "batch", None),
            P("batch"),
            P("side", "batch", None, "mp"),
            P("side", None, ("mp", "batch")),
            P("side", ("mp", "batch"), None),
            P("side", "batch"),
            P("side", "batch"),
            P("side", "batch"),
            P("side", "batch", "mp"),
            P("side", ("mp", "batch")),
            P("side", ("mp", "batch"), None),
            P("side", "batch"),
            P("side", "batch"),
            P("side", "batch"),
        ),
        check_vma=False,
    )
```

```python
import functools
import types

import jax
import jax.numpy as jnp
from jax import lax
from jax.experimental import pallas as pl
from jax.experimental.pallas import tpu as pltpu
from jax.sharding import PartitionSpec as P

MESH = pl.DeviceIdType.MESH
bf16 = jnp.bfloat16
f32 = jnp.float32
WIDTH = 768
HALF = 384
ROWS = 768
SLOT = 64
SLOTS = 12
PAIRS = 6
EPS = 1e-05
SIM_SCALE = 0.1


def nn(a, b):
    return lax.dot_general(a, b, (((1,), (0,)), ((), ())), preferred_element_type=f32)


def nt(a, b):
    return lax.dot_general(a, b, (((1,), (1,)), ((), ())), preferred_element_type=f32)


def tn(a, b):
    return lax.dot_general(a, b, (((0,), (0,)), ((), ())), preferred_element_type=f32)


def iota(shape, axis):
    return lax.broadcasted_iota(jnp.int32, shape, axis)


def split_pair(block):
    first = iota(block.shape, 1) < 64
    zero = jnp.zeros_like(block)
    return jnp.concatenate([jnp.where(first, block, zero), jnp.where(first, zero, block)], axis=0)


def merge_pair(stacked):
    rows = stacked.shape[0] // 2
    first = iota((rows, 128), 1) < 64
    return jnp.where(first, stacked[:rows], stacked[rows:])


def mean_of(values):
    return jnp.sum(values, axis=1, keepdims=True) * (1.0 / WIDTH)


def norm_back(d, n, gain, root):
    u = d * gain
    return (u - mean_of(u) - n * mean_of(u * n)) * root


def partial_sum(values):
    return jnp.sum(values.reshape(values.shape[0] // 8, 8, values.shape[1]), axis=0)


def column_sum(values):
    return jnp.sum(values, axis=0, keepdims=True)


class Counter:
    def __init__(self):
        self.n = 0

    def take(self):
        self.n += 1
        return self.n - 1


class Bundle:
    def __init__(self, group, where, first, grad, r1, r2, r3, finish, apart):
        self.first, self.grad, self.finish, self.apart = first, grad, finish, apart
        self.r1, self.r2, self.r3 = r1, r2, r3
        self.x, self.y, self.z, self.device = where
        self.a = self.y if first == "y" else self.x
        self.b = self.x if first == "y" else self.y
        self.last = grad.shape[2] if first == "y" else grad.shape[0]
        self.step = 0
        far = r3.at[pl.ds(0, self.last)], r3.at[pl.ds(4, 3)]
        self.landing = (r1, r2) + (far if apart else (r3,))
        self.group = [group() for _ in self.landing]

    def index(self, a, z, b):
        return (a, z, b) if self.first == "y" else (b, z, a)

    def piece(self, a, z):
        return self.grad.at[a, z] if self.first == "y" else self.grad.at[:, z, a]

    def to(self, da, dz, db):
        return self.device(da, dz, db) if self.first == "y" else self.device(db, dz, da)

    def owner_b(self, b):
        return b if self.last == 4 else b // 2

    def send(self, step, src, dst, to):
        self.group[step](src, dst, to).start()

    def wait(self, step):
        self.group[step](self.landing[step], self.landing[step], self.to(1, 0, 0)).wait_recv()

    def add(self, where, others):
        def step(k, carry):
            totals = []
            for b in (k * 2, k * 2 + 1):
                total = self.grad[where(b)].astype(f32)
                for ref, index in others(b):
                    total = total + ref[index].astype(f32)
                totals.append(total.astype(bf16))
            for b, total in enumerate(totals):
                self.grad[where(k * 2 + b)] = total
            return carry

        lax.fori_loop(0, self.last // 2, step, 0)

    def advance(self):
        if self.apart:
            (self.step0, self.step1, self.step2z, self.step3z, self.step4)[self.step]()
        else:
            (self.step0, self.step1, self.step2, self.step4)[self.step]()
        self.step += 1

    def done(self):
        return self.step == len(self.landing) + 1

    def step0(self):
        far, up, down = (self.a + 2) % 4, (self.a + 1) % 4, (self.a + 3) % 4
        self.send(0, self.piece(far, 0), self.r1.at[0], self.to(1, 0, 0))
        self.send(0, self.piece(far, 1), self.r1.at[1], self.to(3, 0, 0))
        self.send(1, self.piece(up, 1), self.r2.at[0, 1], self.to(1, 0, 0))
        self.send(1, self.piece(down, 0), self.r2.at[1, 0], self.to(3, 0, 0))

    def step1(self):
        self.wait(0)
        for way, near in ((0, (self.a + 1) % 4), (1, (self.a + 3) % 4)):
            self.add(lambda b: self.index(near, way, b), lambda b: [(self.r1, (way, b))])
            self.send(1, self.piece(near, way), self.r2.at[way, way], self.to((1, 3)[way], 0, 0))

    def own_quarter(self, z):
        self.add(lambda b: self.index(self.a, z, b), lambda b: [(self.r2, (way, z, b)) for way in range(2)])

    def step2(self):
        self.wait(1)
        for z in range(2):
            self.own_quarter(z)
        for dz, db in ((1, 2), (1, 1), (1, 3), (0, 2), (1, 0), (0, 1), (0, 3)):
            src = self.grad.at[self.index(self.a, (self.z + dz) % 2, self.owner_b((self.b + db) % 4))]
            self.send(2, src, self.r3.at[dz * 4 + db - 1], self.to(0, dz, db))

    def step2z(self):
        self.wait(1)
        self.own_quarter(1 - self.z)
        self.send(2, self.piece(self.a, 1 - self.z), self.landing[2], self.to(0, 1, 0))
        self.own_quarter(self.z)

    def step3z(self):
        self.wait(2)
        self.add(lambda b: self.index(self.a, self.z, b), lambda b: [(self.r3, (b,))])
        for db in (2, 1, 3):
            src = self.grad.at[self.index(self.a, self.z, self.owner_b((self.b + db) % 4))]
            self.send(3, src, self.r3.at[3 + db], self.to(0, 0, db))

    def step4(self):
        self.wait(len(self.landing) - 1)
        for part in range(self.grad.shape[3] // 16):
            rows = pl.ds(part * 16, 16)
            total = self.grad[self.index(self.a, self.z, self.owner_b(self.b)) + (rows,)].astype(f32)
            for k in range(4, 7) if self.apart else range(7):
                total = total + self.r3[k, rows].astype(f32)
            self.finish(part, total)

    def drain(self):
        for step, landing in enumerate(self.landing):
            self.group[step](landing, landing, self.to(1, 0, 0)).wait_send()


def layer_kernel(n_copies, near_in, names, *refs):
    r = types.SimpleNamespace(**dict(zip(names, refs)))
    side, batch, core = lax.axis_index("side"), lax.axis_index("batch"), lax.axis_index("mp")
    y, z, x = batch // 8, (batch // 4) % 2, batch % 4

    def device(dy, dz, dx):
        return (side, ((y + dy) % 4) * 8 + ((z + dz) % 2) * 4 + (x + dx) % 4, core)

    def across(dx):
        return (1 - side, y * 8 + z * 4 + (x + dx) % 4, core)

    mate = (side, batch, 1 - core)
    count = Counter()
    local = Counter()
    open_sends = []

    def rc(src, dst, to):
        k = count.take()
        return pltpu.make_async_remote_copy(
            src_ref=src, dst_ref=dst, send_sem=r.send.at[k], recv_sem=r.recv.at[k], device_id=to, device_id_type=MESH
        )

    def group():
        k = count.take()

        def make(src, dst, to):
            return pltpu.make_async_remote_copy(
                src_ref=src, dst_ref=dst, send_sem=r.send.at[k], recv_sem=r.recv.at[k], device_id=to, device_id_type=MESH
            )

        return make

    def to_mate(src, dst):
        copy = rc(src, dst, mate)
        copy.start()
        open_sends.append(copy)
        return copy

    def fetch(src, dst):
        copy = pltpu.make_async_copy(src, dst, r.lsem.at[local.take()])
        copy.start()
        return copy

    hid, wqkv, wout, wup, wdown, qkv = r.hid, r.wqkv, r.wout, r.wup, r.wdown, r.qkv
    own_rows = pl.ds(pl.multiple_of(core * ROWS, ROWS), ROWS)

    barrier = pltpu.get_barrier_semaphore()
    steps = [(dy, dz, 0) for dy in range(4) for dz in range(2)] + [(0, dz, dx) for dz in range(2) for dx in (1, 2, 3)]
    greeted = [mate] + [device(*step) for step in steps[1:]] + [across(dx) for dx in range(4)]
    for to in greeted:
        pl.semaphore_signal(barrier, inc=1, device_id=to, device_id_type=MESH)
    got_lengths = fetch(r.far_lengths, r.lengths)
    got_near = {name: fetch(getattr(r, "far_" + name), getattr(r, name)) for name in near_in}
    got_hid = fetch(r.far_hidden_in.at[own_rows], hid)
    got_qkv = [fetch(r.far_w_qkv.at[p], wqkv.at[p, :, pl.ds(0, HALF)]) for p in range(3)]

    mask = r.mask
    got_lengths.wait()
    for slot in range(SLOTS):
        count_live = r.lengths[core * SLOTS + slot]
        live = iota((SLOT, 256), 0) < count_live
        seen = ((iota((SLOT, 256), 1) // SLOT) == (slot % 4)) | (iota((SLOT, 256), 1) < 256 * side)
        mask[pl.ds(slot * SLOT, SLOT), :] = jnp.where(live & seen, 0.0, -1000000000.0).astype(bf16)

    for copy in got_near.values():
        copy.wait()
    r.bias_qv[0] = r.b_qv[...]
    r.bias_up[0] = r.b_up[...]
    got_hid.wait()

    def project(p, half):
        cols = pl.ds(half * HALF, HALF)
        value = nn(hid[...], wqkv[p, :, cols])
        if p == 0:
            value = (value + r.bias_qv[half, 0:1, :]).astype(bf16) * jnp.asarray(0.125, bf16)
        if p == 2:
            value = value + r.bias_qv[half, 1:2, :]
        qkv[p, :, cols] = value.astype(bf16)

    for p in range(3):
        got_qkv[p].wait()
        project(p, 0)
    pl.semaphore_wait(barrier, len(greeted))
    new_qkv = [to_mate(r.far_w_qkv.at[p], wqkv.at[p, :, pl.ds(HALF, HALF)]) for p in range(3)]
    new_qv = to_mate(r.far_b_qv, r.bias_qv.at[1])
    new_bias = to_mate(r.far_b_up, r.bias_up.at[1])
    got_out = fetch(r.far_w_out, wout.at[pl.ds(0, HALF)])
    got_up = fetch(r.far_w_up, wup.at[0])
    got_down = fetch(r.far_w_down, wdown.at[0])
    got_grad = fetch(r.far_out_grad.at[core], r.stage)

    ctx, weights = r.ctx, r.weights

    def attend(pair, carry):
        cols = pl.ds(pl.multiple_of(pair * 128, 128), 128)
        for tile in range(3):
            rows = pl.ds(tile * 256, 256)
            scores = nt(split_pair(qkv[1, rows, cols]), qkv[0, rows, cols])
            parts = []
            for h in range(2):
                s = scores[h * 256 : (h + 1) * 256] + mask[rows, :].astype(f32)
                e = jnp.exp(s - jnp.max(s, axis=0, keepdims=True))
                parts.append((e * (1.0 / jnp.sum(e, axis=0, keepdims=True))).astype(bf16))
            w = jnp.concatenate(parts, axis=0)
            weights[pair * 3 + tile] = w
            ctx[rows, cols] = tn(w, split_pair(qkv[2, rows, cols])).astype(bf16)
        return carry

    lax.fori_loop(0, 2, attend, 0)
    for copy in new_qkv:
        copy.wait_send()
    open_sends[:] = [copy for copy in open_sends if not any(copy is other for other in new_qkv)]
    new_out = to_mate(r.far_w_out, wout.at[pl.ds(HALF, HALF)])
    new_up = to_mate(r.far_w_up, wup.at[1])
    new_down = to_mate(r.far_w_down, wdown.at[1])
    lax.fori_loop(2, 3, attend, 0)
    new_qv.wait_recv()
    for p in range(3):
        new_qkv[p].wait_recv()
        project(p, 1)
    lax.fori_loop(3, PAIRS, attend, 0)

    cls, line, landed, back, sgrad = r.cls, r.line, r.landed, r.back, r.sgrad
    r.cls_in[...] = jnp.zeros_like(r.cls_in)
    for slot in range(SLOTS):
        rows = pl.ds(slot * SLOT, 16)
        r.cls_in[0, slot : slot + 1, :] = ctx[rows, :].astype(f32)[0:1]
        r.cls_in[1, slot : slot + 1, :] = hid[rows, :].astype(f32)[0:1]
    got_out.wait()
    new_out.wait_recv()
    v = nn(r.cls_in[0].astype(bf16), wout[...]) + r.cls_in[1] + r.b_out[...]
    v = v - mean_of(v)
    v = v * lax.rsqrt(mean_of(v * v) + EPS) * r.ln1_gain[...] + r.ln1_bias[...]
    r.cls_low[...] = v.astype(bf16)
    cls[...] = v + r.b_down[...]
    got_up.wait()
    got_down.wait()
    new_up.wait_recv()
    new_down.wait_recv()
    new_bias.wait_recv()

    def feed_cls(j, carry):
        half, part = j // 3, j % 3
        inner = pl.ds(pl.multiple_of(part * 512, 512), 512)
        u = nn(r.cls_low[...], wup[half, :, inner]) + r.bias_up[half, :, inner]
        a = (u * (0.5 + 0.5 * lax.erf(u * 0.7071067811865476))).astype(bf16)
        cls[...] += nn(a, wdown[half, part].reshape(512, WIDTH))
        return carry

    lax.fori_loop(0, 6, feed_cls, 0)
    v = cls[...]
    v = v - mean_of(v)
    v = v * lax.rsqrt(mean_of(v * v) + EPS) * r.ln2_gain[...] + r.ln2_bias[...]
    cls[...] = v.astype(bf16).astype(f32)

    shifts = [(dy, dz) for dy in range(4) for dz in range(2)][1:]
    here = y * 2 + z
    give = [rc(r.mine, line.at[x], across(dx)) for dx in range(4)]
    spread = [rc(r.around, landed.at[here], device(dy, dz, 0)) for dy, dz in shifts]
    gather = [rc(landed.at[((y + dy) % 4) * 2 + ((z + dz) % 2)], r.terms.at[here], device(dy, dz, 0)) for dy, dz in shifts]
    hand = [rc(back.at[(x + dx) % 4], line.at[x], across(dx)) for dx in range(4)]
    swap_p = rc(r.given.at[0], r.given.at[1], mate)
    swap_q = rc(r.ques.at[0], r.ques.at[1], mate)
    send_loss = rc(r.loss, r.loss, across(0))
    sgrad[...] = jnp.zeros_like(sgrad)

    @pl.when(side == 1)
    def _():
        for t in range(3):
            r.mine[pl.ds(t, 1), :] = cls[pl.ds(t * 4, 1), :]
        r.mine[pl.ds(3, 1), :] = cls[pl.ds(0, 1), :]
        for copy in give:
            copy.start()

    @pl.when(side == 0)
    def _():
        r.ques[0] = cls[...].astype(bf16)
        swap_q.start()

    def loss_spread():
        for copy in give:
            copy.wait_recv()
        r.around[...] = line[...].reshape(16, WIDTH).astype(bf16)
        for copy in spread:
            copy.start()
        landed[here] = r.around[...]

    def loss_swap():
        for copy in spread:
            copy.wait_recv()
        r.given[0] = landed[...].reshape(128, WIDTH)
        swap_p.start()

    def loss_values():
        swap_q.wait_recv()
        place = iota((32, 32), 0)
        home = (place // SLOTS) ^ core
        wanted = home * 16 + place % SLOTS
        picks = ((iota((32, 32), 1) == wanted) & (place < 24)).astype(bf16)
        questions = nn(picks, r.ques[...].reshape(32, WIDTH))[0:24]
        swap_p.wait_recv()
        col = iota((192, 256), 0)
        chip, inner = col // 6, col % 6
        owner = inner // 3
        spot = (owner ^ core) * 128 + chip * 4 + inner % 3
        picks = (iota((192, 256), 1) == spot).astype(bf16)
        passages = nn(picks, r.given[...].reshape(256, WIDTH))
        sims = nt(questions.astype(bf16), passages.astype(bf16)) * SIM_SCALE
        chosen = r.positives[...] > 0
        top = jnp.max(sims, axis=1, keepdims=True)
        lse_all = top + jnp.log(jnp.sum(jnp.exp(sims - top), axis=1, keepdims=True))
        picked = jnp.where(chosen, sims, -1000000000.0)
        top_pos = jnp.max(picked, axis=1, keepdims=True)
        lse_pos = top_pos + jnp.log(jnp.sum(jnp.exp(picked - top_pos), axis=1, keepdims=True))
        r.loss[...] = jnp.broadcast_to(lse_all - lse_pos, (24, 128))
        send_loss.start()
        gap = jnp.exp(sims - lse_all) - jnp.where(chosen, jnp.exp(picked - lse_pos), 0.0)
        gap = gap * SIM_SCALE
        col = iota((192, 128), 1)
        source = (col // 4) * 6 + core * 3 + col % 4
        picks = ((iota((192, 128), 0) == source) & (col % 4 < 3)).astype(bf16)
        high = gap.astype(bf16)
        gaps = (high, (gap - high.astype(f32)).astype(bf16))
        rows, all_passages = questions.astype(bf16), passages.astype(bf16)
        total = sum(tn(nn(part, picks).astype(bf16), rows) for part in gaps)
        for copy in spread:
            copy.wait_send()
        landed[...] = total.astype(bf16).reshape(8, 16, WIDTH)
        for copy in gather:
            copy.start()
        sgrad[...] = sum(nn(part, all_passages) for part in gaps)
        r.terms[here] = landed[here]

    def loss_hand():
        for copy in gather:
            copy.wait_recv()
        back[...] = jnp.sum(r.terms[...].astype(f32), axis=0).reshape(4, 4, WIDTH)
        for copy in hand:
            copy.start()

    def loss_back():
        @pl.when(side == 1)
        def _():
            for copy in hand:
                copy.wait_recv()
            summed = jnp.sum(line[...], axis=0)
            for t in range(3):
                sgrad[pl.ds(core * SLOTS + t * 4, 1), :] = summed[t : t + 1]
            send_loss.wait_recv()
            for copy in give:
                copy.wait_send()

        @pl.when(side == 0)
        def _():
            for copy in gather + hand + [swap_p, swap_q, send_loss]:
                copy.wait_send()


    n1, roots, low1, f = r.n1, r.roots, r.low1, r.f
    f[...] = nn(ctx[...], wout[...])

    def first_norm(chunk, carry):
        rows = pl.ds(pl.multiple_of(chunk * 256, 256), 256)
        v = f[rows, :] + hid[rows, :].astype(f32) + r.b_out[...]
        v = v - mean_of(v)
        root = lax.rsqrt(mean_of(v * v) + EPS)
        n = v * root
        n1[rows, :] = n.astype(bf16)
        roots[rows, 0:1] = root
        h1 = n * r.ln1_gain[...] + r.ln1_bias[...]
        low1[rows, :] = h1.astype(bf16)
        f[rows, :] = h1 + r.b_down[...]
        return carry

    lax.fori_loop(0, 3, first_norm, 0)

    act, slope = r.act, r.slope

    def feed(j, carry):
        half, block = j // 3, j % 3
        pl.when((side == 0) & (j == 1))(loss_spread)
        pl.when((side == 0) & (j == 4))(loss_swap)
        pl.when((side == 0) & (j == 5))(loss_values)
        inner = pl.ds(pl.multiple_of(block * 512, 512), 512)
        cols = pl.ds(pl.multiple_of(j * 512, 512), 512)
        u = nn(low1[...], wup[half, :, inner]) + r.bias_up[half, :, inner]
        for part in range(6):
            rows = pl.ds(part * 128, 128)
            v = u[part * 128 : (part + 1) * 128]
            cdf = 0.5 + 0.5 * lax.erf(v * 0.7071067811865476)
            bell = jnp.exp(v * v * -0.5) * 0.3989422804014327
            act[rows, cols] = (v * cdf).astype(bf16)
            slope[rows, cols] = (cdf + v * bell).astype(bf16)
        a = act[:, cols]
        for part in range(3):
            out = pl.ds(part * 256, 256)
            f[:, out] += nn(a, wdown[half, block, :, :, :, :, out].reshape(512, 256))
        return carry

    lax.fori_loop(0, 6, feed, 0)

    low2 = r.d_low

    def second_norm(chunk, carry):
        rows = pl.ds(pl.multiple_of(chunk * 256, 256), 256)
        v = f[rows, :]
        v = v - mean_of(v)
        root = lax.rsqrt(mean_of(v * v) + EPS)
        n = v * root
        f[rows, :] = n
        roots[rows, 1:2] = root
        e = (n * r.ln2_gain[...] + r.ln2_bias[...]).astype(bf16)
        low2[rows, :] = e
        return carry

    lax.fori_loop(0, 3, second_norm, 0)
    put_encoded = fetch(low2, r.far_encoded.at[own_rows])
    mate_encoded = to_mate(low2, r.far_encoded.at[own_rows])

    pl.when(side == 0)(loss_hand)
    loss_back()
    puts = [fetch(r.loss, r.far_loss)]

    d_low, sums, og = r.d_low, r.sums, r.stage
    put_encoded.wait()
    mate_encoded.wait_send()
    open_sends[:] = [copy for copy in open_sends if copy is not mate_encoded]
    got_grad.wait()
    sums[...] = jnp.zeros_like(sums)

    def second_back(block, carry):
        rows = pl.ds(pl.multiple_of(block * 192, 192), 192)
        whole = og[block // 2, block % 2].reshape(192, WIDTH)
        place = iota((SLOT, WIDTH), 0)
        parts = []
        for part in range(3):
            slot = block * 3 + part
            count_live = r.lengths[core * SLOTS + slot]
            lead = jnp.where((side == 1) & (slot % 4 != 0), 0, 1)
            keep = (place < count_live) & (place >= lead)
            d = jnp.where(keep, whole[part * SLOT : (part + 1) * SLOT].astype(f32), 0.0)
            parts.append(d + jnp.where(place == 0, sgrad[pl.ds(core * SLOTS + slot, 1), :], 0.0))
        d = jnp.concatenate(parts, axis=0)
        n = f[rows, :]
        sums[0] += partial_sum(d * n)
        sums[1] += partial_sum(d)
        d = norm_back(d, n, r.ln2_gain[...], roots[rows, 1:2])
        sums[2] += partial_sum(d)
        f[rows, :] = d
        d_low[rows, :] = d.astype(bf16)
        return carry

    lax.fori_loop(0, 4, second_back, 0)

    where = (x, y, z, device)
    stage = r.stage
    bundles = []

    def start(name, grad, first, finish, apart=False):
        got = [getattr(r, part + name) for part in ("r1_", "r2_", "r3_")]
        b = Bundle(group, where, first, grad, *got, finish, apart)
        bundles.append(b)
        b.advance()
        return b

    def columns(ref, first):
        return ref.at[:, :, :, :, pl.ds(first, HALF)]

    def send_half(name, blocks, make, slot):
        grad = getattr(r, "g_" + name)
        per = 4 // blocks
        moves = []
        for k in range(blocks):
            value = make(1, k).astype(bf16)
            if k > 0:
                moves[k - 1].wait_send()
            slot[...] = value
            moves.append(rc(slot, grad.at[pl.ds(k * per, per)], mate))
            moves[k].start()
        return moves

    def keep_half(name, make, moves):
        grad = getattr(r, "g_" + name)
        per = 4 // len(moves)
        for k, move in enumerate(moves):
            span = pl.ds(k * per, per)
            value = make(0, k)
            move.wait_recv()
            grad[span] = (value + grad[span].astype(f32)).astype(bf16)
        moves[-1].wait_send()

    def make_down(half, k):
        cols = pl.ds(half * 1536 + k * 768, 768)
        return tn(act[:, cols], d_low[...]).reshape(2, 2, 4, 48, WIDTH)

    def end_down(first):
        def finish(part, total):
            r.g_w_down[pl.ds(part * 16, 16), pl.ds(first, HALF)] = total

        return finish

    moves = send_half("down", 2, make_down, stage)

    def feed_back(j, carry):
        half, part = j // 3, j % 3
        inner = pl.ds(pl.multiple_of(part * 512, 512), 512)
        cols = pl.ds(pl.multiple_of(j * 512, 512), 512)
        value = nt(d_low[...], wdown[half, part].reshape(512, WIDTH))
        d = (value * slope[:, cols].astype(f32)).astype(bf16)
        slope[:, cols] = d
        r.sum_up[:, cols] = column_sum(partial_sum(d.astype(f32)))
        for part in range(3):
            out = pl.ds(part * 256, 256)
            f[:, out] += nt(d, wup[half, out, inner])
        return carry

    lax.fori_loop(3, 5, feed_back, 0)
    keep_half("down", make_down, moves)
    down = [
        start("downa", columns(r.g_down, 0), "x", end_down(0), True),
        start("downb", columns(r.g_down, HALF), "y", end_down(HALF), True),
    ]
    lax.fori_loop(5, 6, feed_back, 0)

    def make_up(half, k):
        value = tn(low1[:, pl.ds(k * 384, 384)], slope[:, pl.ds(half * 1536, 1536)])
        left = value[:, :768].reshape(48, 8, WIDTH)
        right = value[:, 768:].reshape(48, 8, WIDTH)
        return jnp.concatenate([left, right], axis=1).reshape(2, 2, 4, 48, WIDTH)

    def end_up(first):
        def finish(part, total):
            rows = pl.ds(part * 8, 8)
            r.g_w_up[rows, pl.ds(first, HALF)] = total[:8]
            r.g_w_up[rows, pl.ds(768 + first, HALF)] = total[8:]

        return finish

    moves = send_half("up", 2, make_up, stage)
    lax.fori_loop(0, 2, feed_back, 0)
    for b in down:
        b.advance()
    lax.fori_loop(2, 3, feed_back, 0)
    pl.semaphore_signal(r.free, inc=1, device_id=mate, device_id_type=MESH)
    keep_half("up", make_up, moves)
    up = [
        start("upa", columns(r.g_up, 0), "x", end_up(0), True),
        start("upb", columns(r.g_up, HALF), "y", end_up(HALF), True),
    ]

    def first_back(chunk, carry):
        rows = pl.ds(pl.multiple_of(chunk * 256, 256), 256)
        d = f[rows, :]
        n = n1[rows, :].astype(f32)
        sums[3] += partial_sum(d * n)
        sums[4] += partial_sum(d)
        d = norm_back(d, n, r.ln1_gain[...], roots[rows, 0:1])
        sums[5] += partial_sum(d)
        f[rows, :] = d
        d_low[rows, :] = d.astype(bf16)
        return carry

    lax.fori_loop(0, 3, first_back, 0)
    for b in down:
        b.advance()

    def make_out(half, k):
        value = tn(ctx[:, pl.ds(half * HALF, HALF)], d_low[...])
        left = value[:, :HALF].reshape(48, 8, HALF)
        right = value[:, HALF:].reshape(48, 8, HALF)
        return jnp.concatenate([left, right], axis=1).reshape(4, 2, 2, 48, HALF)

    def end_out(part, total):
        rows = pl.ds(part * 8, 8)
        r.g_w_out[rows, pl.ds(0, HALF)] = total[:8]
        r.g_w_out[rows, pl.ds(HALF, HALF)] = total[8:]

    moves = send_half("out", 1, make_out, r.stage_out)
    act[:, 0:WIDTH] = nt(d_low[...], wout[...]).astype(bf16)

    def pair_back(pair):
        cols = pl.ds(pl.multiple_of(pair * 128, 128), 128)

        results = []
        for tile in range(3):
            rows = pl.ds(tile * 256, 256)
            q, k, d = qkv[0, rows, cols], qkv[1, rows, cols], act[rows, cols]
            w = weights[pair * 3 + tile]
            dw = nt(split_pair(qkv[2, rows, cols]), d)
            parts = []
            for h in range(2):
                wh = w[h * 256 : (h + 1) * 256].astype(f32)
                dh = dw[h * 256 : (h + 1) * 256]
                parts.append((wh * (dh - column_sum(wh * dh))).astype(bf16))
            ds = jnp.concatenate(parts, axis=0)
            results.append(
                (
                    (tn(ds, split_pair(k)) * 0.125).astype(bf16),
                    merge_pair(nn(ds, q)).astype(bf16),
                    merge_pair(nn(w, d)).astype(bf16),
                )
            )
        for tile in range(3):
            for p in range(3):
                qkv[p, pl.ds(tile * 256, 256), cols] = results[tile][p]
        for k, p in ((6, 0), (7, 2)):
            sums[k, :, cols] = sum(partial_sum(results[tile][p].astype(f32)) for tile in range(3))

    def make_qkv(pair):
        cols = pl.ds(pair * 128, 128)
        d = jnp.concatenate([qkv[p, :, cols] for p in range(3)], axis=1)
        value = tn(hid[...], d).reshape(32, 24, HALF)
        a, b, c = value[:, 0:8], value[:, 8:16], value[:, 16:24]
        top = jnp.concatenate([a, b[:, :, :256]], axis=2)
        low = jnp.concatenate([b[:, :, 256:], c, jnp.zeros((32, 8, 128), f32)], axis=2)
        return jnp.concatenate([top, low], axis=1).reshape(4, 2, 4, 16, 640)

    def end_qkv(pair, first):
        def finish(part, total):
            r.sum_qkv[pair, :, pl.ds(first, total.shape[1])] = total

        return finish

    grad_qkv = [wdown.at[1, k, :, :, :, :, pl.ds(0, 640)] for k in range(3)]
    stage_qkv = [wdown.at[0, k, :, :, :, :, pl.ds(0, 640)] for k in range(3)]
    moves_qkv = [rc(stage_qkv[k], grad_qkv[k], mate) for k in range(3)]
    pl.semaphore_wait(r.free, 1)
    for k in range(3):
        pair_back(3 + k)
        stage_qkv[k][...] = make_qkv(3 + k).astype(bf16)
        moves_qkv[k].start()
        if k == 0:
            keep_half("out", make_out, moves)
            out = start("out", r.g_out, "y", end_out)
    last = []
    for k in range(3):
        pair_back(k)
        value = make_qkv(k)
        moves_qkv[k].wait_recv()
        grad_qkv[k][...] = (value + grad_qkv[k][...].astype(f32)).astype(bf16)
        for part, first, start_col, width in (("a", "x", 0, HALF), ("b", "y", HALF, 256)):
            view = wdown.at[1, k, :, :, :, :, pl.ds(start_col, width)]
            last.append(start("qkv%d" % k + part, view, first, end_qkv(k, start_col)))
        for b in (up + down, [out], up)[k]:
            b.advance()
    for k in range(3):
        moves_qkv[k].wait_send()

    vec = r.vec

    def pack(half):
        up = r.sum_up[:, pl.ds(half * 1536, 1536)]
        cols = pl.ds(half * HALF, HALF)
        qv = jnp.concatenate([column_sum(sums[6, :, cols]), column_sum(sums[7, :, cols])], axis=1)
        common = [column_sum(sums[k]) for k in range(6)]
        return jnp.concatenate([up[:, :768], up[:, 768:], qv] + common + [jnp.zeros((7, WIDTH), f32)], axis=0)

    vec[0] = pack(1)
    vec[1] = pack(0)
    vec_mate = to_mate(vec.at[0], vec.at[2])
    vec_state = {}

    def vec_go(buffer, place, ways):
        copies = []
        for way in ways:
            copy = rc(buffer.at[place], buffer.at[place], device(*way))
            copy.start()
            open_sends.append(copy)
            copies.append(copy)
        vec_state["open"] = copies

    def vec_wait():
        for copy in vec_state["open"]:
            copy.wait_recv()

    f[...] += nt(qkv[0], wqkv[0])
    vec_mate.wait_recv()
    r.vec_x[x] = vec[1] + vec[2]
    vec_go(r.vec_x, x, [(0, 0, dx) for dx in (1, 2, 3)])
    for b in last[0:4]:
        b.advance()
    f[...] += nt(qkv[1], wqkv[1])
    for b in [out] + down:
        b.advance()
    ctx[...] = (f[...] + nt(qkv[2], wqkv[2])).astype(bf16)
    put_grad = fetch(ctx, r.far_input_grad.at[own_rows])
    mate_grad = to_mate(ctx, r.far_input_grad.at[own_rows])
    for b in last[4:6]:
        b.advance()
    vec_wait()
    r.vec_yz[here] = jnp.sum(r.vec_x[...], axis=0)
    vec_go(r.vec_yz, here, [(dy, dz, 0) for dy, dz in shifts])
    for b in last[0:4] + up + last[4:6] + [out] + last[0:4] + up + last[4:6]:
        b.advance()
    vec_wait()
    r.g_vec[...] = jnp.sum(r.vec_yz[...], axis=0)
    for k in range(3):
        t = r.sum_qkv[k]
        top, low = t[:8], t[8:]
        whole = jnp.concatenate(
            [top[:, :HALF], jnp.concatenate([top[:, HALF:], low[:, :128]], axis=1), low[:, 128:512]], axis=0
        )
        for p in range(3):
            r.g_w_qkv[p, :, pl.ds(k * 128, 128)] = whole[:, p * 128 : (p + 1) * 128]
    puts += [fetch(getattr(r, name), getattr(r, "far_" + name)) for name in ("g_w_qkv", "g_w_out", "g_w_up", "g_w_down", "g_vec")]
    put_grad.wait()
    for copy in puts:
        copy.wait()
    mate_grad.wait_recv()
    mate_encoded.wait_recv()
    for copy in open_sends:
        copy.wait_send()
    assert all(b.done() for b in bundles)
    for b in bundles:
        b.drain()
    assert count.n <= n_copies and local.n <= 26


N_COPIES = 91


def layer(lengths, far_in, near_in):
    far = pl.BlockSpec(memory_space=pl.ANY)
    outs = dict(
        encoded=((1536, WIDTH), bf16),
        input_grad=((1536, WIDTH), bf16),
        loss=((24, 128), f32),
        g_w_qkv=((3, 24, HALF), f32),
        g_w_out=((24, WIDTH), f32),
        g_w_up=((24, 1536), f32),
        g_w_down=((48, WIDTH), f32),
        g_vec=((16, WIDTH), f32),
    )
    scratch = dict(
        hid=((ROWS, WIDTH), bf16),
        wqkv=((3, WIDTH, WIDTH), bf16),
        wout=((WIDTH, WIDTH), bf16),
        wup=((2, WIDTH, 1536), bf16),
        wdown=((2, 3, 4, 2, 4, 16, WIDTH), bf16),
        qkv=((3, ROWS, WIDTH), bf16),
        weights=((18, 512, 256), bf16),
        ctx=((ROWS, WIDTH), bf16),
        n1=((ROWS, WIDTH), bf16),
        low1=((ROWS, WIDTH), bf16),
        act=((ROWS, 3072), bf16),
        slope=((ROWS, 3072), bf16),
        f=((ROWS, WIDTH), f32),
        d_low=((ROWS, WIDTH), bf16),
        roots=((ROWS, 2), f32),
        mask=((ROWS, 256), bf16),
        bias_qv=((2, 2, HALF), f32),
        bias_up=((2, 1, 1536), f32),
        cls=((16, WIDTH), f32),
        mine=((4, WIDTH), f32),
        cls_in=((2, 16, WIDTH), f32),
        cls_low=((16, WIDTH), bf16),
        line=((4, 4, WIDTH), f32),
        back=((4, 4, WIDTH), f32),
        around=((16, WIDTH), bf16),
        landed=((8, 16, WIDTH), bf16),
        terms=((8, 16, WIDTH), bf16),
        sum_qkv=((3, 16, 640), f32),
        g_down=((4, 2, 4, 48, WIDTH), bf16),
        g_up=((4, 2, 4, 48, WIDTH), bf16),
        g_out=((4, 2, 2, 48, HALF), bf16),
        given=((2, 128, WIDTH), bf16),
        ques=((2, 16, WIDTH), bf16),
        sgrad=((24, WIDTH), f32),
        sums=((8, 8, WIDTH), f32),
        sum_up=((1, 3072), f32),
        stage=((2, 2, 4, 48, WIDTH), bf16),
        stage_out=((4, 2, 2, 48, HALF), bf16),
        vec=((3, 16, WIDTH), f32),
        vec_x=((4, 16, WIDTH), f32),
        vec_yz=((8, 16, WIDTH), f32),
    )

    def buffers(name, last, rows, cols):
        scratch["r1_" + name] = ((2, last, rows, cols), bf16)
        scratch["r2_" + name] = ((2, 2, last, rows, cols), bf16)
        scratch["r3_" + name] = ((7, rows, cols), bf16)

    for part in "ab":
        buffers("down" + part, 4, 48, HALF)
        buffers("up" + part, 4, 48, HALF)
        for k in range(3):
            buffers("qkv%d" % k + part, 4, 16, HALF if part == "a" else 256)
    buffers("out", 2, 48, HALF)
    sems = dict(
        send=pltpu.SemaphoreType.DMA((N_COPIES,)),
        recv=pltpu.SemaphoreType.DMA((N_COPIES,)),
        lsem=pltpu.SemaphoreType.DMA((26,)),
        free=pltpu.SemaphoreType.REGULAR,
    )
    for name, value in near_in.items():
        scratch[name] = (value.shape, value.dtype)
    for name, (shape, kind) in outs.items():
        if kind == f32:
            scratch[name] = (shape, kind)
    sems["lengths"] = pltpu.SMEM(lengths.shape, jnp.int32)
    names = ["far_" + name for name in ["lengths"] + list(far_in) + list(near_in) + list(outs)] + list(scratch) + list(sems)
    results = pl.pallas_call(
        functools.partial(layer_kernel, N_COPIES, list(near_in), names),
        name="layer",
        out_shape=[jax.ShapeDtypeStruct(shape, kind) for shape, kind in outs.values()],
        in_specs=[far] * (1 + len(far_in) + len(near_in)),
        out_specs=[far] * len(outs),
        scratch_shapes=[pltpu.VMEM(shape, kind) for shape, kind in scratch.values()] + list(sems.values()),
        compiler_params=pltpu.CompilerParams(
            collective_id=0, has_side_effects=True, vmem_limit_bytes=VMEM_LIMIT
        ),
    )(lengths, *far_in.values(), *near_in.values())
    return types.SimpleNamespace(**dict(zip(outs, results)))


VMEM_LIMIT = 64 * 1024 * 1024 - 256 * 1024


def finish_kernel(copies, names, *refs):
    r = types.SimpleNamespace(**dict(zip(names, refs)))
    batch = lax.axis_index("batch")
    near = []
    for name in ("vec", "w_out", "losses"):
        copy = pltpu.make_async_copy(getattr(r, name), getattr(r, "near_" + name), r.sems.at[0, 12 + len(near)])
        copy.start()
        near.append(copy)
    moves = []
    for name in copies:
        src, hold, dst = getattr(r, name), getattr(r, "hold_" + name), getattr(r, "out_" + name)
        parts = 4 if src.shape[0] == 1536 else 1
        rows = src.shape[0] // parts
        for part in range(parts):
            span, k = pl.ds(part * rows, rows), len(moves)
            first = pltpu.make_async_copy(src.at[span], hold.at[span], r.sems.at[0, k])
            first.start()
            moves.append((first, pltpu.make_async_copy(hold.at[span], dst.at[span], r.sems.at[1, k])))
    for first, second in moves:
        first.wait()
        second.start()
    for copy in near:
        copy.wait()
    common = pltpu.roll(r.near_vec[...], (WIDTH - batch * 24) % WIDTH, 1)
    for k, ref in enumerate((r.ln2_gain, r.ln2_bias, r.b_down, r.ln1_gain, r.ln1_bias, r.b_out)):
        ref[...] = common[3 + k : 4 + k, 0:24]
    up = pltpu.roll(r.near_vec[...], (WIDTH - (batch % 16) * 48) % WIDTH, 1)
    r.b_up[...] = jnp.where(batch < 16, up[0:1, 0:48], up[1:2, 0:48])
    qv = pltpu.roll(r.near_vec[...], (WIDTH - batch * 12) % WIDTH, 1)
    r.b_qv[0:1, :] = qv[2:3, 0:12]
    r.b_qv[1:2, :] = qv[2:3, HALF : HALF + 12]
    for k in range(12):
        r.out_w_out[k] = r.near_w_out[pl.ds((batch % 2) * 12 + k, 1), :]
    diagonal = iota((24, 128), 0) == iota((24, 128), 1)
    r.loss[...] = column_sum(jnp.where(diagonal, r.near_losses[...], 0.0))[:, 0:24]
    for _, second in moves:
        second.wait()


def finish(out):
    far, vmem = pl.BlockSpec(memory_space=pl.ANY), pl.BlockSpec(memory_space=pltpu.VMEM)
    large = dict(encoded=out.encoded, input_grad=out.input_grad, w_qkv=out.g_w_qkv, w_up=out.g_w_up, w_down=out.g_w_down)
    small = dict(vec=out.g_vec, w_out=out.g_w_out, losses=out.loss)
    row = jax.ShapeDtypeStruct((1, 24), f32)
    results = dict(
        out_w_out=jax.ShapeDtypeStruct((12, 1, WIDTH), f32),
        b_qv=jax.ShapeDtypeStruct((2, 12), f32),
        b_up=jax.ShapeDtypeStruct((1, 48), f32),
        b_down=row,
        b_out=row,
        ln1_gain=row,
        ln1_bias=row,
        ln2_gain=row,
        ln2_bias=row,
        loss=row,
    )
    moved = {"out_" + name: jax.ShapeDtypeStruct(value.shape, value.dtype) for name, value in large.items()}
    names = list(large) + list(small) + list(moved) + list(results) + ["hold_" + name for name in large] + ["near_" + name for name in small] + ["sems"]
    values = pl.pallas_call(
        functools.partial(finish_kernel, list(large), names),
        name="finish",
        out_shape=list(moved.values()) + list(results.values()),
        in_specs=[far] * (len(large) + len(small)),
        out_specs=[far] * len(moved) + [vmem] * len(results),
        scratch_shapes=[pltpu.VMEM(value.shape, value.dtype) for value in (large | small).values()] + [pltpu.SemaphoreType.DMA((2, 16))],
        compiler_params=pltpu.CompilerParams(vmem_limit_bytes=VMEM_LIMIT),
    )(*large.values(), *small.values())
    return types.SimpleNamespace(**dict(zip(list(moved) + list(results), values)))


def on_device(
    hidden_in, w_qkv, b_qv, w_out, b_out, ln1_gain, ln1_bias, w_up, b_up, w_down, b_down, ln2_gain, ln2_bias, lengths, positives, out_grad
):
    out = layer(
        lengths[0],
        dict(
            hidden_in=hidden_in[0],
            w_qkv=jnp.transpose(w_qkv[0], (1, 0, 2)),
            w_out=w_out[0],
            w_up=w_up[0],
            w_down=w_down[0].reshape(3, 4, 2, 4, 16, WIDTH),
            out_grad=out_grad[0].reshape(2, 2, 2, 4, 48, WIDTH),
        ),
        dict(
            b_qv=b_qv[0],
            b_up=b_up,
            b_out=b_out,
            ln1_gain=ln1_gain,
            ln1_bias=ln1_bias,
            b_down=b_down,
            ln2_gain=ln2_gain,
            ln2_bias=ln2_bias,
            positives=positives,
        ),
    )
    out = finish(out)
    return (
        out.out_encoded[None],
        out.out_input_grad[None],
        out.loss[0],
        jnp.transpose(out.out_w_qkv, (1, 0, 2))[None],
        out.b_qv[None],
        jnp.transpose(out.out_w_out, (1, 0, 2)),
        out.b_out,
        out.ln1_gain,
        out.ln1_bias,
        out.out_w_up[None],
        out.b_up,
        out.out_w_down[None],
        out.b_down,
        out.ln2_gain,
        out.ln2_bias,
    )


def solution(mesh):
    placed = (
        P("side", "batch", None),
        P("side", None, None, "mp"),
        P("side", None, "mp"),
        P("side", "mp", None),
        P("side", None),
        P("side", None),
        P("side", None),
        P("side", None, "mp"),
        P("side", "mp"),
        P("side", "mp", None),
        P("side", None),
        P("side", None),
        P("side", None),
        P("side", "batch"),
        P("batch", None),
        P("side", "batch", None),
    )
    return jax.shard_map(
        on_device,
        mesh=mesh,
        in_specs=placed,
        out_specs=(
            P("side", "batch", None),
            P("side", "batch", None),
            P("batch"),
            P("side", "batch", None, "mp"),
            P("side", None, ("mp", "batch")),
            P("side", ("mp", "batch"), None),
            P("side", "batch"),
            P("side", "batch"),
            P("side", "batch"),
            P("side", "batch", "mp"),
            P("side", ("mp", "batch")),
            P("side", ("mp", "batch"), None),
            P("side", "batch"),
            P("side", "batch"),
            P("side", "batch"),
        ),
        check_vma=False,
    )
```
